512 devices in a mesh: frame: 32 (over x_lo, z), head: 16 (over y, x_hi, core).
Axes of the slice: x: 4 (x_hi: 2, x_lo: 2; x = x_hi * 2 + x_lo), y: 4, z: 16, core: 2. Of those that a mesh axis runs over, the one named last changes fastest.
Arguments:
- query_rows: bfloat16 [12288, 6144], P('frame', 'head'), may hold values from -15 to 15
- key_rows: bfloat16 [12288, 6144], P('frame', 'head'), may hold values from -15 to 15
- value_rows: bfloat16 [12288, 6144], P('frame', 'head'), may hold values from -6 to 6
- windows: int32 [24, 3], replicated, may hold values from 0 to 1
- out_weight: bfloat16 [3072, 3072], P('head'), may hold values from -0.109375 to 0.109375
Outputs:
- mixed: bfloat16 [2, 12288, 3072], P(None, ('frame', 'head'))
The draws below stay inside these ranges and needn't reach their ends.
All inputs are finite; a program needn't handle non-finite values.
Results may differ from the reference program's by a relative error of at most 0.0062.
Values may be sent and summed in bfloat16 or wider, within the bound.
A program may use at most 64 MiB of HBM per device.

```python
import math
import jax
import jax.numpy as jnp
from jax import lax

D = 3072
HEADS = 24
HD = 128
SEEDS = 2
TILE_F = 6
TILE_H = 8
TILE_W = 4
FRAME_TILES = 4
WT = 2
TOK_DEV = 384
TOKENS = 12288
HEADS_DEV = 3
N_FRAME = 32
N_HEAD = 16


def draw_query_rows(key, part):
    key = jax.random.fold_in(key, 5)
    array_shape = (TOKENS, SEEDS * HEADS * HD)
    drawn_rows = jax.random.truncated_normal(key, -4.0, 4.0, array_shape, jnp.float32)
    return drawn_rows.astype(jnp.bfloat16)


def draw_key_rows(key, part):
    key = jax.random.fold_in(key, 7)
    array_shape = (TOKENS, SEEDS * HEADS * HD)
    drawn_rows = jax.random.truncated_normal(key, -4.0, 4.0, array_shape, jnp.float32)
    return drawn_rows.astype(jnp.bfloat16)


def set_ends(drawn, key, smallest, top_value):
    index_at = [jax.random.randint(jax.random.fold_in(key, axis), (), 0, length) for axis, length in enumerate(drawn.shape)]
    main_axis = drawn.shape.index(max(drawn.shape))
    next_to = index_at[:main_axis] + [(index_at[main_axis] + 1) % drawn.shape[main_axis]] + index_at[main_axis + 1:]
    return drawn.at[tuple(index_at)].set(smallest).at[tuple(next_to)].set(top_value)


def levels(stream_key, shape, pieces, least, largest):
    def one(position, shards_of):
        heights = jax.random.uniform(jax.random.fold_in(jax.random.fold_in(stream_key, 6), position), (shards_of,), jnp.float32, least / len(pieces), largest / len(pieces))
        return jnp.repeat(jnp.exp(heights), shape[position] // shards_of).reshape((-1,) + (1,) * (len(shape) - position - 1))

    gain = one(*pieces[0])
    for cut in pieces[1:]:
        gain = gain * one(*cut)
    return gain


def scatter_about(rng, dims, scale, most, cuts=(), kind=jnp.bfloat16):
    drawn = scale * jax.random.normal(rng, dims, jnp.float32)
    if cuts:
        drawn = drawn * levels(rng, dims, cuts, -0.22, 0.18)
    return jnp.clip(drawn, -most, most).astype(kind)


def setup_inputs(seed: int = 0) -> dict:
    streams_of = jax.random.split(jax.random.key(seed), 6)
    return {
        "query_rows": draw_query_rows(jax.random.fold_in(streams_of[5], 71), 0),
        "key_rows": draw_key_rows(jax.random.fold_in(streams_of[5], 71), 0),
        "value_rows": scatter_about(streams_of[2], (TOKENS, SEEDS * HEADS * HD), 1.0, 6.0, ((0, 32), (1, 16))),
        "windows": set_ends(jax.random.randint(streams_of[3], (HEADS, 3), 0, 2), jax.random.fold_in(streams_of[3], 1), 0, 1).astype(jnp.int32),
        "out_weight": scatter_about(streams_of[4], (HEADS * HD, D), (HEADS * HD) ** -0.5, 0.109375, ((0, 16),)),
    }


NEGATIVE = -1e+30

def reorder(block_rows, row_total, groups):
    shaped = block_rows.reshape(row_total, groups, SEEDS, HEADS_DEV, HD)
    return jnp.transpose(shaped, (0, 2, 1, 3, 4)).reshape(row_total, SEEDS, HEADS, HD)

def reference(query_rows, key_rows, value_rows, windows, out_weight):
    tile_size = TILE_F * TILE_H * TILE_W
    row_tiles = N_FRAME // FRAME_TILES
    groups = N_HEAD // SEEDS
    scaling = 1.0 / math.sqrt(HD)
    width_all = SEEDS * HEADS * HD
    counter = jnp.arange(WT, dtype=jnp.int32)
    col_near = jnp.abs(counter[:, None] - counter[None, :])
    step_list = jnp.array([-1, -1, -1, 0, 0, 0, 1, 1, 1], dtype=jnp.int32)
    row_list = jnp.array([-1, 0, 1, -1, 0, 1, -1, 0, 1], dtype=jnp.int32)
    key_grid = jnp.pad(key_rows.reshape(FRAME_TILES, row_tiles, TOK_DEV, width_all), ((1, 1), (1, 1), (0, 0), (0, 0)))
    value_grid = jnp.pad(value_rows.reshape(FRAME_TILES, row_tiles, TOK_DEV, width_all), ((1, 1), (1, 1), (0, 0), (0, 0)))
    weight_groups = out_weight.astype(jnp.float32).reshape(groups, HEADS_DEV * HD, D)

    def one_block(block_index):
        frame_tile = (block_index // row_tiles).astype(jnp.int32)
        tile_row = (block_index % row_tiles).astype(jnp.int32)
        row_start = (block_index * TOK_DEV).astype(jnp.int32)
        zero = jnp.int32(0)
        local_query = reorder(lax.dynamic_slice_in_dim(query_rows, row_start, TOK_DEV, 0).astype(jnp.float32), TOK_DEV, groups)
        near_keys = reorder(lax.dynamic_slice(key_grid, (frame_tile, tile_row, zero, zero), (3, 3, TOK_DEV, width_all)).astype(jnp.float32), 9 * TOK_DEV, groups)
        near_values = reorder(lax.dynamic_slice(value_grid, (frame_tile, tile_row, zero, zero), (3, 3, TOK_DEV, width_all)).astype(jnp.float32), 9 * TOK_DEV, groups)
        present = (frame_tile + step_list >= 0) & (frame_tile + step_list < FRAME_TILES) & (tile_row + row_list >= 0) & (tile_row + row_list < row_tiles)
        allowed = (jnp.abs(step_list)[None, None, :, None] <= windows[:, 0][:, None, None, None]) & (jnp.abs(row_list)[None, None, :, None] <= windows[:, 1][:, None, None, None]) & (col_near[None, :, None, :] <= windows[:, 2][:, None, None, None]) & present[None, None, :, None]
        scores = jnp.einsum('qshd,kshd->shqk', local_query, near_keys) * scaling
        scores = scores.reshape(SEEDS, HEADS, WT, tile_size, 9, WT, tile_size)
        scores = jnp.where(allowed[None, :, :, None, :, :, None], scores, NEGATIVE)
        scores = scores.reshape(SEEDS, HEADS, TOK_DEV, 9 * TOK_DEV)
        row_peak = lax.optimization_barrier(jnp.max(scores, axis=-1, keepdims=True))
        weights = jnp.exp(scores - row_peak)
        denominator = lax.optimization_barrier(jnp.sum(weights, axis=-1))
        rounded = lax.optimization_barrier(weights.astype(jnp.bfloat16)).astype(jnp.float32)
        attended = jnp.einsum('shqk,kshd->qshd', rounded, near_values) / jnp.transpose(denominator, (2, 0, 1))[..., None]
        attended = attended.astype(jnp.bfloat16)
        grouped = attended.reshape(TOK_DEV, SEEDS, groups, HEADS_DEV * HD).astype(jnp.float32)
        group_part = jnp.einsum('qsgc,gcd->sgqd', grouped, weight_groups)
        group_part = lax.optimization_barrier(group_part.astype(jnp.bfloat16)).astype(jnp.float32)
        return lax.optimization_barrier(jnp.sum(group_part, axis=1)).astype(jnp.bfloat16)
    blocks = lax.map(one_block, jnp.arange(N_FRAME, dtype=jnp.int32))
    return jnp.transpose(blocks, (1, 0, 2, 3)).reshape(SEEDS, TOKENS, D)
```

```python
import math

import jax
import jax.numpy as jnp
from jax import lax
from jax.experimental import pallas as pl
from jax.experimental.pallas import tpu as pltpu
from jax.sharding import PartitionSpec as P

HD = 128
SEEDS = 2
FRAME_TILES = 4
NEGATIVE = -1e30
MESH = pl.DeviceIdType.MESH
BF = jnp.bfloat16
F32 = jnp.float32

Z, Y = 16, 4
ROW_TILES = 8
HEADS_DEV = 3
TOK = 384
TILE = 192
D = 3072
W_ROWS = 192
OWN = 24
QUARTER = 96

CHAIN, OPPOSITE, FAR, FAR_SAME, FAR_LAST, ACROSS = 0, 1, 2, 3, 4, 5
KINDS = 8


def kernel(q_hbm, k_hbm, v_hbm, windows, w_hbm, out_ref, *scratch):
    (kv, q_s, w_all, att, att_all, acc_o, send_o, recv_o, m_s, l_s, acc_s) = scratch[:11]
    (local_sem, z_send, z_recv, y_send, y_recv, w_send, w_recv, f_send, f_recv) = scratch[11:]

    frame = lax.axis_index("frame")
    head = lax.axis_index("head")
    xl, z = frame // Z, frame % Z
    y, xh, c = head // 4, (head // 2) % 2, head % 2
    row = z % ROW_TILES
    upper = z // ROW_TILES
    step = 2 * c - 1
    forwards = upper == xl

    def at_z(distance):
        return (xl * Z + (z + distance + Z) % Z, head)

    def at_y(distance):
        return (frame, ((y + distance) % Y) * 4 + xh * 2 + c)

    across_x = ((1 - xl) * Z + z, head)
    other_core = (frame, y * 4 + xh * 2 + 1 - c)

    def at_final(k):
        return (frame, y * 4 + (xh + k // 2) % 2 * 2 + (c + k) % 2)

    def local_copies(h):
        cols = pl.ds(pl.multiple_of(h * HD, HD), HD)
        return [
            pltpu.make_async_copy(k_hbm.at[:, cols], kv.at[0, h, 0], local_sem.at[0, h]),
            pltpu.make_async_copy(v_hbm.at[:, cols], kv.at[0, h, 1], local_sem.at[1, h]),
            pltpu.make_async_copy(q_hbm.at[:, cols], q_s.at[h], local_sem.at[2, h]),
        ]

    my_rows = pl.ds(pl.multiple_of(c * W_ROWS, W_ROWS), W_ROWS)
    w_local = pltpu.make_async_copy(w_hbm, w_all.at[y, my_rows], local_sem.at[3, 0])
    for h in range(HEADS_DEV):
        for copy in local_copies(h):
            copy.start()
    w_local.start()

    barrier = pltpu.get_barrier_semaphore()
    partners = [at_z(1), at_z(-1), at_z(6), at_z(-6), across_x]
    partners += [at_y(1), at_y(2), at_y(3), at_final(1), at_final(2), at_final(3)]
    for partner in partners:
        pl.semaphore_signal(barrier, inc=1, device_id=partner, device_id_type=MESH)
    pl.semaphore_wait(barrier, len(partners))

    def remote(src, dst, send, recv, target):
        return pltpu.make_async_remote_copy(
            src_ref=src, dst_ref=dst, send_sem=send, recv_sem=recv, device_id=target, device_id_type=MESH
        )

    def z_copy(kind, h):
        source, slot, target = {
            CHAIN: (0, 2, at_z(step)),
            OPPOSITE: (0, 1, at_z(-step)),
            FAR: (2, 3, at_z(6 * step)),
            FAR_SAME: (3, 4, at_z(step)),
            FAR_LAST: (4, 5, at_z(step)),
            ACROSS: (3, 6, across_x),
            ACROSS + 1: (4, 7, across_x),
            ACROSS + 2: (5, 8, across_x),
        }[kind]
        return remote(kv.at[source, h], kv.at[slot, h], z_send.at[kind, h], z_recv.at[kind, h], target)

    def w_copy(k):
        return remote(w_hbm, w_all.at[y, my_rows], w_send.at[k], w_recv.at[k], at_y(k))

    def w_share(k):
        place = w_all.at[(y + Y - k) % Y, my_rows]
        return remote(place, place, w_send.at[Y + k], w_recv.at[Y + k], other_core)

    def y_copy(k, h):
        rows = pl.ds(pl.multiple_of((y + k) % Y * QUARTER, QUARTER), QUARTER)
        return remote(att.at[h, rows], att_all.at[y, h], y_send.at[k, h], y_recv.at[k, h], at_y(k))

    def f_copy(k, half):
        piece = (xh + k // 2) % 2 * 2 + (c + k) % 2
        return remote(
            send_o.at[half, piece], recv_o.at[half, k], f_send.at[half, k], f_recv.at[half, k], at_final(k)
        )

    for h in range(HEADS_DEV):
        for copy in local_copies(h):
            copy.wait()
        z_copy(CHAIN, h).start()
    for h in range(HEADS_DEV):
        z_copy(OPPOSITE, h).start()
    for k in range(1, Y):
        w_copy(k).start()
    w_local.wait()
    w_share(0).start()
    z_copy(CHAIN, 0).wait_recv()
    z_copy(FAR, 0).start()

    group = y * 2 + xh
    scaling = 1.0 / math.sqrt(HD)
    column = lax.broadcasted_iota(jnp.int32, (1, TOK), 1) // TILE

    def attend(h, slot, far_frame, far_row, first=False):
        head_id = group * HEADS_DEV + h
        allowed = (far_frame <= windows[head_id, 0]) & (far_row <= windows[head_id, 1])
        same = jnp.where(allowed, 0.0, NEGATIVE)
        other = jnp.where(allowed & (windows[head_id, 2] >= 1), 0.0, NEGATIVE)
        keys, values = kv[slot, h, 0], kv[slot, h, 1]
        for half in range(2):
            rows = pl.ds(half * TILE, TILE)
            bias = jnp.where(column == half, same, other)
            scores = lax.dot_general(
                q_s[h, rows], keys, (((1,), (1,)), ((), ())), preferred_element_type=F32
            )
            scores = scores * scaling + bias
            peak = jnp.max(scores, axis=1, keepdims=True)
            if not first:
                before = m_s[rows, :1]
                peak = jnp.maximum(peak, before)
            weights = jnp.exp(scores - peak)
            total = jnp.sum(weights, axis=1, keepdims=True)
            mixed = jnp.dot(weights.astype(BF), values, preferred_element_type=F32)
            if not first:
                fade = jnp.exp(before - peak)
                total += fade * l_s[rows, :1]
                mixed += fade * acc_s[rows]
            m_s[rows] = jnp.broadcast_to(peak, (TILE, HD))
            l_s[rows] = jnp.broadcast_to(total, (TILE, HD))
            acc_s[rows] = mixed

    def in_grid(r):
        return (r >= 0) & (r < ROW_TILES)

    ahead, behind = in_grid(row + step), in_grid(row - step)

    def one_head(h, carry):
        attend(h, 0, 0, 0, first=True)
        z_copy(OPPOSITE, h).wait_recv()

        @pl.when(behind)
        def _():
            attend(h, 2, 0, 1)

        @pl.when(ahead)
        def _():
            attend(h, 1, 0, 1)

        z_copy(FAR, h).wait_recv()
        z_copy(FAR_SAME, h).start()

        @pl.when(h < HEADS_DEV - 1)
        def _():
            z_copy(CHAIN, h + 1).wait_recv()
            z_copy(FAR, h + 1).start()

        @pl.when(forwards)
        def _():
            z_copy(ACROSS, h).start()

        @pl.when(ahead)
        def _():
            attend(h, 3, 1, 1)

        z_copy(FAR_SAME, h).wait_recv()
        z_copy(FAR_LAST, h).start()

        @pl.when(forwards)
        def _():
            z_copy(ACROSS + 1, h).start()

        attend(h, 4, 1, 0)
        z_copy(FAR_LAST, h).wait_recv()

        @pl.when(forwards)
        def _():
            z_copy(ACROSS + 2, h).start()

        @pl.when(behind)
        def _():
            attend(h, 5, 1, 1)

        @pl.when(h == HEADS_DEV - 1)
        def _():
            project_early()

        @pl.when(jnp.logical_not(forwards))
        def _():
            z_copy(ACROSS, h).wait_recv()

            @pl.when(ahead)
            def _():
                attend(h, 6, 1, 1)

            z_copy(ACROSS + 1, h).wait_recv()
            attend(h, 7, 1, 0)
            z_copy(ACROSS + 2, h).wait_recv()

            @pl.when(behind)
            def _():
                attend(h, 8, 1, 1)

        att[h] = (acc_s[...] / l_s[...]).astype(BF)
        for k in range(1, Y):
            y_copy(k, h).start()
        att_all[y, h] = att[h, pl.ds(pl.multiple_of(y * QUARTER, QUARTER), QUARTER)]
        return carry

    wide = D // 6

    def project_early():
        for k in range(1, Y):
            w_copy(k).wait_recv()
            w_share(k).start()
        for k in range(Y):
            w_share(k).wait_recv()
        for k in range(1, Y):
            for h in range(HEADS_DEV - 1):
                y_copy(k, h).wait_recv()
        depth = (HEADS_DEV - 1) * HD

        def part(i, carry):
            cols = pl.ds(pl.multiple_of(i * wide, wide), wide)
            total = jnp.zeros((QUARTER, wide), F32)
            for s in range(Y):
                rows = jnp.concatenate([att_all[s, h] for h in range(HEADS_DEV - 1)], axis=1)
                total += jnp.dot(rows, w_all[s, :depth, cols], preferred_element_type=F32)
            acc_o[:, cols] = total
            return carry

        lax.fori_loop(0, 6, part, 0)

    lax.fori_loop(0, HEADS_DEV, one_head, 0)

    last = HEADS_DEV - 1
    for k in range(1, Y):
        y_copy(k, last).wait_recv()
    half_wide, part_wide = D // 2, D // 4
    for half in range(2):
        for piece_col in range(2):
            cols = pl.ds(half * half_wide + piece_col * part_wide, part_wide)
            total = acc_o[:, cols]
            for s in range(Y):
                total += jnp.dot(
                    att_all[s, last], w_all[s, last * HD : (last + 1) * HD, cols], preferred_element_type=F32
                )
            for piece in range(4):
                send_o[half, piece, piece_col * OWN : (piece_col + 1) * OWN, :] = total[
                    piece * OWN : (piece + 1) * OWN
                ].astype(BF)
        for k in (2, 3, 1):
            f_copy(k, half).start()

    own = xh * 2 + c
    for half in range(2):
        for k in range(1, 4):
            f_copy(k, half).wait_recv()
        mine = send_o[half, own].astype(F32) + recv_o[half, 2].astype(F32)
        others = recv_o[half, 1].astype(F32) + recv_o[half, 3].astype(F32)
        mine, others = mine.astype(BF), others.astype(BF)
        for piece_col in range(2):
            cols = pl.ds(half * half_wide + piece_col * part_wide, part_wide)
            rows = slice(piece_col * OWN, (piece_col + 1) * OWN)
            out_ref[0, :, cols] = jnp.where(c == 0, mine[rows], others[rows])
            out_ref[1, :, cols] = jnp.where(c == 0, others[rows], mine[rows])

    def sent(h, carry):
        for kind in range(ACROSS):
            z_copy(kind, h).wait_send()

        @pl.when(forwards)
        def _():
            for kind in range(ACROSS, KINDS):
                z_copy(kind, h).wait_send()

        for k in range(1, Y):
            y_copy(k, h).wait_send()
        return carry

    lax.fori_loop(0, HEADS_DEV, sent, 0)
    for k in range(1, Y):
        w_copy(k).wait_send()
    for k in range(Y):
        w_share(k).wait_send()
    for half in range(2):
        for k in range(1, 4):
            f_copy(k, half).wait_send()


def local(query_rows, key_rows, value_rows, windows, out_weight):
    dma = pltpu.SemaphoreType.DMA
    anywhere = pl.BlockSpec(memory_space=pl.ANY)
    return pl.pallas_call(
        kernel,
        out_shape=jax.ShapeDtypeStruct((SEEDS, OWN, D), BF),
        in_specs=[anywhere] * 3 + [pl.BlockSpec(memory_space=pltpu.SMEM), anywhere],
        out_specs=pl.BlockSpec(memory_space=pltpu.VMEM),
        scratch_shapes=[
            pltpu.VMEM((9, HEADS_DEV, 2, TOK, HD), BF),
            pltpu.VMEM((HEADS_DEV, TOK, HD), BF),
            pltpu.VMEM((Y, 2 * W_ROWS, D), BF),
            pltpu.VMEM((HEADS_DEV, TOK, HD), BF),
            pltpu.VMEM((Y, HEADS_DEV, QUARTER, HD), BF),
            pltpu.VMEM((QUARTER, D), F32),
            pltpu.VMEM((2, 4, 2 * OWN, D // 4), BF),
            pltpu.VMEM((2, 4, 2 * OWN, D // 4), BF),
            pltpu.VMEM((TOK, HD), F32),
            pltpu.VMEM((TOK, HD), F32),
            pltpu.VMEM((TOK, HD), F32),
            dma((4, HEADS_DEV)),
            dma((KINDS, HEADS_DEV)),
            dma((KINDS, HEADS_DEV)),
            dma((Y, HEADS_DEV)),
            dma((Y, HEADS_DEV)),
            dma((2 * Y,)),
            dma((2 * Y,)),
            dma((2, 4)),
            dma((2, 4)),
        ],
        compiler_params=pltpu.CompilerParams(
            collective_id=0, has_side_effects=True, vmem_limit_bytes=48 << 20
        ),
        cost_estimate=pl.CostEstimate(
            flops=2 * (2 * HEADS_DEV * TOK * 9 * TOK * HD + TOK * HEADS_DEV * HD * D),
            bytes_accessed=4 << 20,
            transcendentals=HEADS_DEV * TOK * 9 * TOK,
        ),
    )(query_rows, key_rows, value_rows, windows, out_weight)


def solution(mesh):
    placed = (P("frame", "head"), P("frame", "head"), P("frame", "head"), P(), P("head", None))
    return jax.shard_map(
        local,
        mesh=mesh,
        in_specs=placed,
        out_specs=P(None, ("frame", "head"), None),
        check_vma=False,
    )
```

```python
import math

import jax
import jax.numpy as jnp
from jax import lax
from jax.experimental import pallas as pl
from jax.experimental.pallas import tpu as pltpu
from jax.sharding import PartitionSpec as P

HD = 128
SEEDS = 2
FRAME_TILES = 4
NEGATIVE = -1e30
MESH = pl.DeviceIdType.MESH
BF = jnp.bfloat16
F32 = jnp.float32

Z, Y = 16, 4
ROW_TILES = 8
HEADS_DEV = 3
TOK = 384
TILE = 192
D = 3072
W_ROWS = 192
OWN = 24
QUARTER = 96

CHAIN, OPPOSITE, LEAP, FAR, FAR_SAME, FAR_LAST = range(6)
ROUTES = ((0, 2, 1), (0, 1, -1), (2, 3, 3), (3, 4, 3), (4, 5, 1), (5, 6, 1))
SLOTS = 7
PARTS = 4
PART = D // PARTS
LOG2E = math.log2(math.e)


def kernel(q_hbm, k_hbm, v_hbm, windows, w_hbm, out_ref, *scratch):
    (kv, q_s, w_all, att, att_all, acc_o, send_o, recv_o, m_s, l_s, acc_s) = scratch[:11]
    (part_send, part_recv, lse_send, lse_recv) = scratch[11:15]
    (local_sem, z_send, z_recv, x_send, x_recv, y_send, y_recv, w_send, w_recv, f_send, f_recv) = scratch[15:]

    frame = lax.axis_index("frame")
    head = lax.axis_index("head")
    xl, z = frame // Z, frame % Z
    y, xh, c = head // 4, (head // 2) % 2, head % 2
    row = z % ROW_TILES
    upper = z // ROW_TILES
    step = 2 * c - 1
    helps = upper == xl
    helped = upper != xl

    def at_z(distance):
        return (xl * Z + (z + distance + Z) % Z, head)

    def at_y(distance):
        return (frame, ((y + distance) % Y) * 4 + xh * 2 + c)

    across_x = ((1 - xl) * Z + z, head)
    other_core = (frame, y * 4 + xh * 2 + 1 - c)

    def at_final(k):
        return (frame, y * 4 + (xh + k // 2) % 2 * 2 + (c + k) % 2)

    def local_copy(i, h):
        cols = pl.ds(pl.multiple_of(h * HD, HD), HD)
        source = (k_hbm, v_hbm, q_hbm)[i].at[:, cols]
        target = q_s.at[0, h] if i == 2 else kv.at[0, h, i]
        return pltpu.make_async_copy(source, target, local_sem.at[i, h])

    my_rows = pl.ds(pl.multiple_of(c * W_ROWS, W_ROWS), W_ROWS)
    w_local = pltpu.make_async_copy(w_hbm, w_all.at[y, my_rows], local_sem.at[3, 0])
    for i in range(3):
        for h in range(HEADS_DEV):
            local_copy(i, h).start()
    w_local.start()

    barrier = pltpu.get_barrier_semaphore()
    partners = [at_z(1), at_z(-1), at_z(3), at_z(-3), across_x]
    partners += [at_y(1), at_y(2), at_y(3), at_final(1), at_final(2), at_final(3)]
    for partner in partners:
        pl.semaphore_signal(barrier, inc=1, device_id=partner, device_id_type=MESH)
    pl.semaphore_wait(barrier, len(partners))

    def remote(src, dst, send, recv, target):
        return pltpu.make_async_remote_copy(
            src_ref=src, dst_ref=dst, send_sem=send, recv_sem=recv, device_id=target, device_id_type=MESH
        )

    def z_copy(kind, h):
        source, slot, hops = ROUTES[kind]
        return remote(
            kv.at[source, h], kv.at[slot, h], z_send.at[kind, h], z_recv.at[kind, h], at_z(hops * step)
        )

    def x_query(h):
        return remote(q_s.at[0, h], q_s.at[1, h], x_send.at[0, h], x_recv.at[0, h], across_x)

    def x_part(h):
        return remote(part_send.at[h], part_recv.at[h], x_send.at[1, h], x_recv.at[1, h], across_x)

    def x_lse(h):
        return remote(lse_send.at[h], lse_recv.at[h], x_send.at[2, h], x_recv.at[2, h], across_x)

    def w_copy(k):
        return remote(w_hbm, w_all.at[y, my_rows], w_send.at[k], w_recv.at[k], at_y(k))

    def w_share(k):
        place = w_all.at[(y + Y - k) % Y, my_rows]
        return remote(place, place, w_send.at[Y + k], w_recv.at[Y + k], other_core)

    def y_copy(k, h):
        rows = pl.ds(pl.multiple_of((y + k) % Y * QUARTER, QUARTER), QUARTER)
        return remote(att.at[h, rows], att_all.at[y, h], y_send.at[k, h], y_recv.at[k, h], at_y(k))

    def f_copy(k, part):
        piece = (xh + k // 2) % 2 * 2 + (c + k) % 2
        return remote(
            send_o.at[part, piece], recv_o.at[part, k], f_send.at[part, k], f_recv.at[part, k], at_final(k)
        )

    for h in range(HEADS_DEV):
        local_copy(0, h).wait()
        local_copy(1, h).wait()
        z_copy(CHAIN, h).start()
    for h in range(HEADS_DEV):
        z_copy(OPPOSITE, h).start()
    for h in range(HEADS_DEV):
        local_copy(2, h).wait()

        @pl.when(helped)
        def _():
            x_query(h).start()

    for k in range(1, Y):
        w_copy(k).start()
    w_local.wait()
    w_share(0).start()

    group = y * 2 + xh
    scaling = LOG2E / math.sqrt(HD)
    column = lax.broadcasted_iota(jnp.int32, (1, TOK), 1) // TILE

    def attend(owner, h, slot, far_frame, far_row, first=False):
        head_id = group * HEADS_DEV + h
        allowed = (far_frame <= windows[0, head_id]) & (far_row <= windows[1, head_id])
        same = jnp.where(allowed, 0.0, NEGATIVE)
        other = jnp.where(allowed & (windows[2, head_id] >= 1), 0.0, NEGATIVE)
        keys, values = kv[slot, h, 0], kv[slot, h, 1]
        for half in range(2):
            rows = pl.ds(half * TILE, TILE)
            bias = jnp.where(column == half, same, other)
            scores = lax.dot_general(
                q_s[owner, h, rows], keys, (((1,), (1,)), ((), ())), preferred_element_type=F32
            )
            scores = scores * scaling + bias
            peak = jnp.max(scores, axis=1, keepdims=True)
            if not first:
                before = m_s[owner, h, rows, :1]
                peak = jnp.maximum(peak, before)
            weights = jnp.exp2(scores - peak)
            total = jnp.sum(weights, axis=1, keepdims=True)
            mixed = jnp.dot(weights.astype(BF), values, preferred_element_type=F32)
            if not first:
                fade = jnp.exp2(before - peak)
                total += fade * l_s[owner, h, rows, :1]
                mixed += fade * acc_s[owner, h, rows]
            m_s[owner, h, rows] = jnp.broadcast_to(peak, (TILE, HD))
            l_s[owner, h, rows] = jnp.broadcast_to(total, (TILE, HD))
            acc_s[owner, h, rows] = mixed

    def in_grid(r):
        return (r >= 0) & (r < ROW_TILES)

    ahead, behind = in_grid(row + step), in_grid(row - step)

    def each_head(body):
        def run(h, carry):
            body(h)
            return carry

        lax.fori_loop(0, HEADS_DEV, run, 0)

    def hand_on(h):
        z_copy(CHAIN, h).wait_recv()
        z_copy(LEAP, h).start()

    def near(h):
        attend(0, h, 0, 0, 0, first=True)

        @pl.when(behind)
        def _():
            attend(0, h, 2, 0, 1)

    def near_opposite(h):
        z_copy(OPPOSITE, h).wait_recv()

        @pl.when(ahead)
        def _():
            attend(0, h, 1, 0, 1)

    def leap(h):
        z_copy(LEAP, h).wait_recv()
        z_copy(FAR, h).start()

    def far(h):
        z_copy(FAR, h).wait_recv()
        z_copy(FAR_SAME, h).start()

        @pl.when(helps)
        def _():
            x_query(h).wait_recv()
            m_s[1, h] = jnp.full((TOK, HD), NEGATIVE, F32)
            l_s[1, h] = jnp.zeros((TOK, HD), F32)
            acc_s[1, h] = jnp.zeros((TOK, HD), F32)

        @pl.when(ahead)
        def _():
            attend(0, h, 4, 1, 1)

        @pl.when(ahead & helps)
        def _():
            attend(1, h, 4, 1, 1)

    def far_same(h):
        z_copy(FAR_SAME, h).wait_recv()
        z_copy(FAR_LAST, h).start()
        attend(0, h, 5, 1, 0)

        @pl.when(helps)
        def _():
            attend(1, h, 5, 1, 0)

    def far_last(h):
        z_copy(FAR_LAST, h).wait_recv()

        @pl.when(helps & behind)
        def _():
            attend(1, h, 6, 1, 1)

        @pl.when(helps)
        def _():
            part_send[h] = (acc_s[1, h] / l_s[1, h]).astype(BF)
            x_part(h).start()
            lse = m_s[1, h] + jnp.log2(l_s[1, h])
            for block in range(TOK // HD):
                rows = slice(block * HD, (block + 1) * HD)
                lse_send[h, block : block + 1] = lse[rows].T[:1]
            x_lse(h).start()

        @pl.when(behind)
        def _():
            attend(0, h, 6, 1, 1)

        @pl.when(helps)
        def _():
            att[h] = (acc_s[0, h] / l_s[0, h]).astype(BF)
            spread(h)

    def merge(h):
        x_part(h).wait_recv()
        x_lse(h).wait_recv()
        for block in range(TOK // HD):
            rows = slice(block * HD, (block + 1) * HD)
            lse = jnp.broadcast_to(lse_recv[h, block : block + 1], (HD, HD)).T
            before = m_s[0, h, rows]
            peak = jnp.maximum(before, lse)
            fade, share = jnp.exp2(before - peak), jnp.exp2(lse - peak)
            total = fade * l_s[0, h, rows] + share
            mixed = fade * acc_s[0, h, rows] + share * part_recv[h, rows].astype(F32)
            att[h, rows] = (mixed / total).astype(BF)
        spread(h)

    def spread(h):
        for k in range(1, Y):
            y_copy(k, h).start()
        att_all[y, h] = att[h, pl.ds(pl.multiple_of(y * QUARTER, QUARTER), QUARTER)]

    each_head(hand_on)
    each_head(near)
    each_head(near_opposite)
    each_head(leap)
    each_head(far)
    each_head(far_same)
    for k in range(1, Y):
        w_copy(k).wait_recv()
        w_share(k).start()
    each_head(far_last)

    @pl.when(helped)
    def _():
        each_head(merge)

    for k in range(Y):
        w_share(k).wait_recv()
    last = HEADS_DEV - 1

    def project(h, cols):
        rows = pl.ds(pl.multiple_of(h * HD, HD), HD)
        total = jnp.dot(att_all[0, h], w_all[0, rows, cols], preferred_element_type=F32)
        for s in range(1, Y):
            total += jnp.dot(att_all[s, h], w_all[s, rows, cols], preferred_element_type=F32)
        return total

    for h in range(last):
        for k in range(1, Y):
            y_copy(k, h).wait_recv()
        for part in range(PARTS):
            cols = pl.ds(part * PART, PART)
            if h == 0:
                acc_o[:, cols] = project(h, cols)
            else:
                acc_o[:, cols] += project(h, cols)
    for k in range(1, Y):
        y_copy(k, last).wait_recv()
    for part in range(PARTS):
        cols = pl.ds(part * PART, PART)
        total = (acc_o[:, cols] + project(last, cols)).astype(BF)
        for piece in range(4):
            rows = slice(piece * OWN, (piece + 1) * OWN)
            send_o[part, piece, :OWN] = total[rows, : PART // 2]
            send_o[part, piece, OWN:] = total[rows, PART // 2 :]
        for k in (2, 3, 1):
            f_copy(k, part).start()

    own = xh * 2 + c
    for part in range(PARTS):
        for k in range(1, 4):
            f_copy(k, part).wait_recv()
        mine = send_o[part, own].astype(F32) + recv_o[part, 2].astype(F32)
        others = recv_o[part, 1].astype(F32) + recv_o[part, 3].astype(F32)
        mine, others = mine.astype(BF), others.astype(BF)
        for side in range(2):
            cols = pl.ds(part * PART + side * PART // 2, PART // 2)
            rows = slice(side * OWN, (side + 1) * OWN)
            out_ref[0, :, cols] = jnp.where(c == 0, mine[rows], others[rows])
            out_ref[1, :, cols] = jnp.where(c == 0, others[rows], mine[rows])

    def sent(h):
        for kind in range(len(ROUTES)):
            z_copy(kind, h).wait_send()

        @pl.when(helps)
        def _():
            x_part(h).wait_send()
            x_lse(h).wait_send()

        @pl.when(helped)
        def _():
            x_query(h).wait_send()

        for k in range(1, Y):
            y_copy(k, h).wait_send()

    each_head(sent)
    for k in range(1, Y):
        w_copy(k).wait_send()
    for k in range(Y):
        w_share(k).wait_send()
    for part in range(PARTS):
        for k in range(1, 4):
            f_copy(k, part).wait_send()


def local(query_rows, key_rows, value_rows, windows, out_weight):
    dma = pltpu.SemaphoreType.DMA
    anywhere = pl.BlockSpec(memory_space=pl.ANY)
    return pl.pallas_call(
        kernel,
        out_shape=jax.ShapeDtypeStruct((SEEDS, OWN, D), BF),
        in_specs=[anywhere] * 3 + [pl.BlockSpec(memory_space=pltpu.SMEM), anywhere],
        out_specs=pl.BlockSpec(memory_space=pltpu.VMEM),
        scratch_shapes=[
            pltpu.VMEM((SLOTS, HEADS_DEV, 2, TOK, HD), BF),
            pltpu.VMEM((2, HEADS_DEV, TOK, HD), BF),
            pltpu.VMEM((Y, 2 * W_ROWS, D), BF),
            pltpu.VMEM((HEADS_DEV, TOK, HD), BF),
            pltpu.VMEM((Y, HEADS_DEV, QUARTER, HD), BF),
            pltpu.VMEM((QUARTER, D), F32),
            pltpu.VMEM((PARTS, 4, 2 * OWN, PART // 2), BF),
            pltpu.VMEM((PARTS, 4, 2 * OWN, PART // 2), BF),
            pltpu.VMEM((2, HEADS_DEV, TOK, HD), F32),
            pltpu.VMEM((2, HEADS_DEV, TOK, HD), F32),
            pltpu.VMEM((2, HEADS_DEV, TOK, HD), F32),
            pltpu.VMEM((HEADS_DEV, TOK, HD), BF),
            pltpu.VMEM((HEADS_DEV, TOK, HD), BF),
            pltpu.VMEM((HEADS_DEV, 8, HD), F32),
            pltpu.VMEM((HEADS_DEV, 8, HD), F32),
            dma((4, HEADS_DEV)),
            dma((len(ROUTES), HEADS_DEV)),
            dma((len(ROUTES), HEADS_DEV)),
            dma((3, HEADS_DEV)),
            dma((3, HEADS_DEV)),
            dma((Y, HEADS_DEV)),
            dma((Y, HEADS_DEV)),
            dma((2 * Y,)),
            dma((2 * Y,)),
            dma((PARTS, 4)),
            dma((PARTS, 4)),
        ],
        compiler_params=pltpu.CompilerParams(
            collective_id=0, has_side_effects=True, vmem_limit_bytes=60 << 20
        ),
        cost_estimate=pl.CostEstimate(
            flops=2 * (2 * HEADS_DEV * TOK * 9 * TOK * HD + TOK * HEADS_DEV * HD * D),
            bytes_accessed=4 << 20,
            transcendentals=HEADS_DEV * TOK * 9 * TOK,
        ),
    )(query_rows, key_rows, value_rows, windows.T, out_weight)


def solution(mesh):
    placed = (P("frame", "head"), P("frame", "head"), P("frame", "head"), P(), P("head", None))
    return jax.shard_map(
        local,
        mesh=mesh,
        in_specs=placed,
        out_specs=P(None, ("frame", "head"), None),
        check_vma=False,
    )
```

```python
import math

import jax
import jax.numpy as jnp
from jax import lax
from jax.experimental import pallas as pl
from jax.experimental.pallas import tpu as pltpu
from jax.sharding import PartitionSpec as P

HD = 128
SEEDS = 2
FRAME_TILES = 4
NEGATIVE = -1e30
VMEM = 56164352
MESH = pl.DeviceIdType.MESH
BF = jnp.bfloat16
F32 = jnp.float32

Z, Y = 16, 4
ROW_TILES = 8
HEADS_DEV = 3
TOK = 384
TILE = 192
D = 3072
W_ROWS = 192
OWN = 24
QUARTER = 96

CHAIN, OPPOSITE, LEAP, FAR, FAR_SAME, FAR_LAST = range(6)
ROUTES = ((0, 2, 1), (0, 1, -1), (2, 3, 3), (3, 4, 3), (4, 5, 1), (5, 6, 1))
SLOTS = 7
PIECES = 16
PIECE = 32
PARTS = 4
PART = D // PARTS
LOG2E = math.log2(math.e)
ATT, PARTIAL = range(2)


def kernel(q_hbm, k_hbm, v_hbm, windows, w_hbm, out_ref, *scratch):
    (kv, q_s, w_all, m_s, l_s, acc_s, att, part, att_in, part_in, acc_o, send_o, recv_o) = scratch[:13]
    (local_sem, z_send, z_recv, q_send, q_recv, a_send, a_recv, w_send, w_recv, f_send, f_recv) = scratch[13:]

    frame = lax.axis_index("frame")
    head = lax.axis_index("head")
    xl, z = frame // Z, frame % Z
    y, xh, c = head // 4, (head // 2) % 2, head % 2
    row = z % ROW_TILES
    upper = z // ROW_TILES
    step = 2 * c - 1
    helps = upper == xl
    helped = upper != xl

    def at_z(distance):
        return (xl * Z + (z + distance + Z) % Z, head)

    def at_owner(across, k):
        return ((xl + across) % 2 * Z + z, ((y + k) % Y) * 4 + xh * 2 + c)

    across_x = ((1 - xl) * Z + z, head)
    other_core = (frame, y * 4 + xh * 2 + 1 - c)

    def at_final(k):
        return (frame, y * 4 + (xh + k // 2) % 2 * 2 + (c + k) % 2)

    def local_copy(i, h):
        cols = pl.ds(pl.multiple_of(h * HD, HD), HD)
        source = (k_hbm, v_hbm, q_hbm)[i].at[:, cols]
        target = q_s.at[0, h] if i == 2 else kv.at[0, h, i]
        return pltpu.make_async_copy(source, target, local_sem.at[i, h])

    my_rows = pl.ds(pl.multiple_of(c * W_ROWS, W_ROWS), W_ROWS)
    w_local = pltpu.make_async_copy(w_hbm, w_all.at[y, my_rows], local_sem.at[3, 0])
    for i in range(3):
        for h in range(HEADS_DEV):
            local_copy(i, h).start()
    w_local.start()

    barrier = pltpu.get_barrier_semaphore()
    partners = [at_z(1), at_z(-1), at_z(3), at_z(-3), across_x]
    partners += [at_owner(0, 1), at_owner(0, 2), at_owner(0, 3), at_owner(1, 1), at_owner(1, 2), at_owner(1, 3), at_final(1), at_final(2), at_final(3)]
    for partner in partners:
        pl.semaphore_signal(barrier, inc=1, device_id=partner, device_id_type=MESH)
    pl.semaphore_wait(barrier, len(partners))

    def remote(src, dst, send, recv, target):
        return pltpu.make_async_remote_copy(
            src_ref=src, dst_ref=dst, send_sem=send, recv_sem=recv, device_id=target, device_id_type=MESH
        )

    def z_copy(kind, h):
        source, slot, hops = ROUTES[kind]
        return remote(
            kv.at[source, h], kv.at[slot, h], z_send.at[kind, h], z_recv.at[kind, h], at_z(hops * step)
        )

    def x_query(h):
        return remote(q_s.at[0, h], q_s.at[1, h], q_send.at[h], q_recv.at[h], across_x)

    def w_copy(k):
        return remote(w_hbm, w_all.at[y, my_rows], w_send.at[k], w_recv.at[k], at_owner(0, k))

    def w_share(k):
        place = w_all.at[(y + Y - k) % Y, my_rows]
        return remote(place, place, w_send.at[Y + k], w_recv.at[Y + k], other_core)

    def a_copy(kind, k, h):
        pieces = pl.ds((y + k) % Y * 4, 4)
        source, target = ((att, att_in), (part, part_in))[kind]
        sem = (kind, k, h)
        return remote(source.at[h, pieces], target.at[y, h], a_send.at[sem], a_recv.at[sem], at_owner(kind, k))

    def f_copy(k, part):
        piece = (xh + k // 2) % 2 * 2 + (c + k) % 2
        return remote(
            send_o.at[part, piece], recv_o.at[part, k], f_send.at[part, k], f_recv.at[part, k], at_final(k)
        )

    for h in range(HEADS_DEV):
        local_copy(0, h).wait()
        local_copy(1, h).wait()
        z_copy(CHAIN, h).start()
    for h in range(HEADS_DEV):
        z_copy(OPPOSITE, h).start()
    for h in range(HEADS_DEV):
        local_copy(2, h).wait()

        @pl.when(helped)
        def _():
            x_query(h).start()

    for k in range(1, Y):
        w_copy(k).start()
    w_local.wait()
    w_share(0).start()

    group = y * 2 + xh
    scaling = LOG2E / math.sqrt(HD)
    column = lax.broadcasted_iota(jnp.int32, (1, TOK), 1) // TILE

    ones = jnp.ones((TOK, HD), BF)

    def attend(owner, h, slot, far_frame, far_row, first=False):
        head_id = group * HEADS_DEV + h
        allowed = (far_frame <= windows[0, head_id]) & (far_row <= windows[1, head_id])
        same = jnp.where(allowed, 0.0, NEGATIVE)
        other = jnp.where(allowed & (windows[2, head_id] >= 1), 0.0, NEGATIVE)
        keys = kv[slot, h, 0]
        values = jnp.concatenate([kv[slot, h, 1], ones], axis=1)
        for half in range(2):
            rows = pl.ds(half * TILE, TILE)
            bias = jnp.where(column == half, same, other)
            scores = lax.dot_general(
                q_s[owner, h, rows], keys, (((1,), (1,)), ((), ())), preferred_element_type=F32
            )
            scores = scores * scaling + bias
            peak = jnp.max(scores, axis=1, keepdims=True)
            if not first:
                before = m_s[owner, h, rows, :1]
                peak = jnp.maximum(peak, before)
            weights = jnp.exp2(scores - peak)
            mixed = jnp.dot(weights.astype(BF), values, preferred_element_type=F32)
            mixed, total = mixed[:, :HD], mixed[:, HD:]
            if not first:
                fade = jnp.exp2(before - peak)
                total += fade * l_s[owner, h, rows]
                mixed += fade * acc_s[owner, h, rows]
            m_s[owner, h, rows] = jnp.broadcast_to(peak, (TILE, HD))
            l_s[owner, h, rows] = total
            acc_s[owner, h, rows] = mixed

    def in_grid(r):
        return (r >= 0) & (r < ROW_TILES)

    ahead, behind = in_grid(row + step), in_grid(row - step)

    def each_head(body):
        def run(h, carry):
            body(h)
            return carry

        lax.fori_loop(0, HEADS_DEV, run, 0)

    def hand_on(h):
        z_copy(CHAIN, h).wait_recv()
        z_copy(LEAP, h).start()

    def near(h):
        attend(0, h, 0, 0, 0, first=True)

        @pl.when(behind)
        def _():
            attend(0, h, 2, 0, 1)

    def near_opposite(h):
        z_copy(OPPOSITE, h).wait_recv()

        @pl.when(ahead)
        def _():
            attend(0, h, 1, 0, 1)

    def leap(h):
        z_copy(LEAP, h).wait_recv()
        z_copy(FAR, h).start()

    def far(h):
        z_copy(FAR, h).wait_recv()
        z_copy(FAR_SAME, h).start()

        @pl.when(helps)
        def _():
            x_query(h).wait_recv()
            m_s[1, h] = jnp.full((TOK, HD), NEGATIVE, F32)
            l_s[1, h] = jnp.zeros((TOK, HD), F32)
            acc_s[1, h] = jnp.zeros((TOK, HD), F32)

        @pl.when(ahead)
        def _():
            attend(0, h, 4, 1, 1)

        @pl.when(ahead & helps)
        def _():
            attend(1, h, 4, 1, 1)

    def far_same(h):
        z_copy(FAR_SAME, h).wait_recv()
        z_copy(FAR_LAST, h).start()
        attend(0, h, 5, 1, 0)

        @pl.when(helps)
        def _():
            attend(1, h, 5, 1, 0)

    def diagonal(size):
        shape = (size, HD)
        return lax.broadcasted_iota(jnp.int32, shape, 0) == lax.broadcasted_iota(jnp.int32, shape, 1)

    blank = jnp.zeros((PIECES, PIECE - OWN, HD), BF)
    mask = diagonal(OWN)

    def close(target, owner, h):
        mixed = acc_s[owner, h] / l_s[owner, h]
        target[h, :, :OWN] = mixed.reshape(PIECES, OWN, HD).astype(BF)

    def close_lse(target, owner, h):
        lse = m_s[owner, h] + jnp.log2(l_s[owner, h])
        lse = jnp.sum(jnp.where(mask, lse.reshape(PIECES, OWN, HD), 0.0), axis=1, keepdims=True)
        high = lse.astype(BF).astype(F32)
        middle = (lse - high).astype(BF).astype(F32)
        low = lse - high - middle
        place = lax.broadcasted_iota(jnp.int32, (PIECES, PIECE - OWN, HD), 1)
        lines = jnp.where(place == 0, high, jnp.where(place == 1, middle, jnp.where(place == 2, low, 0.0)))
        target[h, :, OWN:] = lines.astype(BF)

    def far_last(h):
        z_copy(FAR_LAST, h).wait_recv()

        @pl.when(helps)
        def _():
            @pl.when(behind)
            def _():
                attend(1, h, 6, 1, 1)

            close(part, 1, h)
            close_lse(part, 1, h)
            for k in (2, 1, 3, 0):
                a_copy(PARTIAL, k, h).start()
            att[h, :, OWN:] = blank

        @pl.when(behind)
        def _():
            attend(0, h, 6, 1, 1)

        close(att, 0, h)

        @pl.when(helped)
        def _():
            close_lse(att, 0, h)

        for k in (2, 1, 3):
            a_copy(ATT, k, h).start()
        att_in[y, h] = att[h, pl.ds(y * 4, 4)]

    def merged(own, other):
        own, other = own.astype(F32), other.astype(F32)

        def lse(piece):
            line = piece[:, OWN : OWN + 1] + piece[:, OWN + 1 : OWN + 2] + piece[:, OWN + 2 : OWN + 3]
            return jnp.sum(jnp.where(mask, line, 0.0), axis=2, keepdims=True)

        first, second = lse(own), lse(other)
        peak = jnp.maximum(first, second)
        first, second = jnp.exp2(first - peak), jnp.exp2(second - peak)
        total = first + second
        return ((first / total) * own[:, :OWN] + (second / total) * other[:, :OWN]).astype(BF)

    each_head(hand_on)
    each_head(near)
    each_head(near_opposite)
    each_head(leap)
    each_head(far)
    each_head(far_same)
    for k in range(1, Y):
        w_copy(k).wait_recv()
        w_share(k).start()
    each_head(far_last)

    for k in range(Y):
        w_share(k).wait_recv()
    last = HEADS_DEV - 1

    def arrived(h):
        for k in range(1, Y):
            a_copy(ATT, k, h).wait_recv()

        @pl.when(helped)
        def _():
            for k in range(Y):
                a_copy(PARTIAL, k, h).wait_recv()
            shape = (PIECES, PIECE, HD)
            joined = merged(att_in[:, h].reshape(shape), part_in[:, h].reshape(shape))
            att_in[:, h, :, :OWN] = joined.reshape(Y, 4, OWN, HD)

    def project(h, cols):
        rows = pl.ds(pl.multiple_of(h * HD, HD), HD)
        total = jnp.zeros((4 * PIECE, PART), F32)
        for s in range(Y):
            total += jnp.dot(
                att_in[s, h].reshape(4 * PIECE, HD), w_all[s, rows, cols], preferred_element_type=F32
            )
        return total

    for h in range(last):
        arrived(h)
        for part_index in range(PARTS):
            cols = pl.ds(part_index * PART, PART)
            if h == 0:
                acc_o[:, cols] = project(h, cols)
            else:
                acc_o[:, cols] += project(h, cols)
    arrived(last)
    for part_index in range(PARTS):
        cols = pl.ds(part_index * PART, PART)
        total = (acc_o[:, cols] + project(last, cols)).astype(BF)
        for piece in range(4):
            mine = total[piece * PIECE : piece * PIECE + OWN]
            send_o[part_index, piece, :OWN] = mine[:, : PART // 2]
            send_o[part_index, piece, OWN:] = mine[:, PART // 2 :]
        for k in (2, 3, 1):
            f_copy(k, part_index).start()

    own = xh * 2 + c
    for part_index in range(PARTS):
        for k in range(1, 4):
            f_copy(k, part_index).wait_recv()
        mine = send_o[part_index, own].astype(F32) + recv_o[part_index, 2].astype(F32)
        others = recv_o[part_index, 1].astype(F32) + recv_o[part_index, 3].astype(F32)
        mine, others = mine.astype(BF), others.astype(BF)
        for side in range(2):
            cols = pl.ds(part_index * PART + side * PART // 2, PART // 2)
            rows = slice(side * OWN, (side + 1) * OWN)
            out_ref[0, :, cols] = jnp.where(c == 0, mine[rows], others[rows])
            out_ref[1, :, cols] = jnp.where(c == 0, others[rows], mine[rows])

    def sent(h):
        for kind in range(len(ROUTES)):
            z_copy(kind, h).wait_send()

        @pl.when(helps)
        def _():
            for k in range(Y):
                a_copy(PARTIAL, k, h).wait_send()

        @pl.when(helped)
        def _():
            x_query(h).wait_send()

        for k in range(1, Y):
            a_copy(ATT, k, h).wait_send()

    each_head(sent)
    for k in range(1, Y):
        w_copy(k).wait_send()
    for k in range(Y):
        w_share(k).wait_send()
    for part_index in range(PARTS):
        for k in range(1, 4):
            f_copy(k, part_index).wait_send()


def local(query_rows, key_rows, value_rows, windows, out_weight):
    dma = pltpu.SemaphoreType.DMA
    anywhere = pl.BlockSpec(memory_space=pl.ANY)
    return pl.pallas_call(
        kernel,
        out_shape=jax.ShapeDtypeStruct((SEEDS, OWN, D), BF),
        in_specs=[anywhere] * 3 + [pl.BlockSpec(memory_space=pltpu.SMEM), anywhere],
        out_specs=pl.BlockSpec(memory_space=pltpu.VMEM),
        scratch_shapes=[
            pltpu.VMEM((SLOTS, HEADS_DEV, 2, TOK, HD), BF),
            pltpu.VMEM((2, HEADS_DEV, TOK, HD), BF),
            pltpu.VMEM((Y, 2 * W_ROWS, D), BF),
            pltpu.VMEM((2, HEADS_DEV, TOK, HD), F32),
            pltpu.VMEM((2, HEADS_DEV, TOK, HD), F32),
            pltpu.VMEM((2, HEADS_DEV, TOK, HD), F32),
            pltpu.VMEM((HEADS_DEV, PIECES, PIECE, HD), BF),
            pltpu.VMEM((HEADS_DEV, PIECES, PIECE, HD), BF),
            pltpu.VMEM((Y, HEADS_DEV, 4, PIECE, HD), BF),
            pltpu.VMEM((Y, HEADS_DEV, 4, PIECE, HD), BF),
            pltpu.VMEM((4 * PIECE, D), F32),
            pltpu.VMEM((PARTS, 4, 2 * OWN, PART // 2), BF),
            pltpu.VMEM((PARTS, 4, 2 * OWN, PART // 2), BF),
            dma((4, HEADS_DEV)),
            dma((len(ROUTES), HEADS_DEV)),
            dma((len(ROUTES), HEADS_DEV)),
            dma((HEADS_DEV,)),
            dma((HEADS_DEV,)),
            dma((2, Y, HEADS_DEV)),
            dma((2, Y, HEADS_DEV)),
            dma((2 * Y,)),
            dma((2 * Y,)),
            dma((PARTS, 4)),
            dma((PARTS, 4)),
        ],
        compiler_params=pltpu.CompilerParams(
            collective_id=0, has_side_effects=True, vmem_limit_bytes=VMEM
        ),
        cost_estimate=pl.CostEstimate(
            flops=2 * (2 * HEADS_DEV * TOK * 9 * TOK * HD + TOK * HEADS_DEV * HD * D),
            bytes_accessed=4 << 20,
            transcendentals=HEADS_DEV * TOK * 9 * TOK,
        ),
    )(query_rows, key_rows, value_rows, windows.T, out_weight)


def solution(mesh):
    placed = (P("frame", "head"), P("frame", "head"), P("frame", "head"), P(), P("head", None))
    return jax.shard_map(
        local,
        mesh=mesh,
        in_specs=placed,
        out_specs=P(None, ("frame", "head"), None),
        check_vma=False,
    )
```

```python
import math

import jax
import jax.numpy as jnp
from jax import lax
from jax.experimental import pallas as pl
from jax.experimental.pallas import tpu as pltpu
from jax.sharding import PartitionSpec as P

HD = 128
SEEDS = 2
FRAME_TILES = 4
NEGATIVE = -1e30
VMEM = 56164352
MESH = pl.DeviceIdType.MESH
BF = jnp.bfloat16
F32 = jnp.float32

Z, Y = 16, 4
ROW_TILES = 8
HEADS_DEV = 3
TOK = 384
TILE = 192
D = 3072
W_ROWS = 192
OWN = 24
QUARTER = 96

CHAIN, OPPOSITE, LEAP, FAR, FAR_SAME, FAR_LAST = range(6)
ROUTES = ((0, 2, 1), (0, 1, -1), (2, 3, 3), (3, 4, 3), (4, 5, 1), (5, 6, 1))
SLOTS = 7
BLOCK = 112
PARTS = 2
PART = D // PARTS
LOG2E = math.log2(math.e)
ATT, PARTIAL = range(2)


def kernel(q_hbm, k_hbm, v_hbm, windows, w_hbm, out_ref, *scratch):
    (kv, q_s, w_all, m_s, l_s, acc_s, att, part, att_in, part_in, acc_o, send_o, recv_o) = scratch[:13]
    (local_sem, z_send, z_recv, q_send, q_recv, a_send, a_recv, w_send, w_recv, f_send, f_recv) = scratch[13:]

    frame = lax.axis_index("frame")
    head = lax.axis_index("head")
    xl, z = frame // Z, frame % Z
    y, xh, c = head // 4, (head // 2) % 2, head % 2
    row = z % ROW_TILES
    upper = z // ROW_TILES
    step = 2 * c - 1
    helps = upper == xl
    helped = upper != xl

    def z_place(distance):
        return (xl * Z + (z + distance + Z) % Z, head)

    z_places = {hops: z_place(hops * step) for hops in (-3, -1, 1, 3)}

    quarters = [(y + k) % Y for k in range(Y)]
    owners = [[((xl + a) % 2 * Z + z, quarter * 4 + xh * 2 + c) for quarter in quarters] for a in range(2)]

    def at_owner(across, k):
        return owners[across][k]

    across_x = ((1 - xl) * Z + z, head)
    other_core = (frame, y * 4 + xh * 2 + 1 - c)

    finals = [(frame, y * 4 + (xh + k // 2) % 2 * 2 + (c + k) % 2) for k in range(4)]

    def at_final(k):
        return finals[k]

    def local_copy(i, h):
        cols = pl.ds(pl.multiple_of(h * HD, HD), HD)
        source = (k_hbm, v_hbm, q_hbm)[i].at[:, cols]
        target = q_s.at[0, h] if i == 2 else kv.at[0, h, i]
        return pltpu.make_async_copy(source, target, local_sem.at[i, h])

    my_rows = pl.ds(pl.multiple_of(c * W_ROWS, W_ROWS), W_ROWS)
    w_local = pltpu.make_async_copy(w_hbm, w_all.at[y, my_rows], local_sem.at[3, 0])
    for i in range(3):
        for h in range(HEADS_DEV):
            local_copy(i, h).start()
    w_local.start()

    barrier = pltpu.get_barrier_semaphore()
    partners = [z_places[1], z_places[-1], z_places[3], z_places[-3], across_x]
    partners += [at_owner(0, 1), at_owner(0, 2), at_owner(0, 3), at_owner(1, 1), at_owner(1, 2), at_owner(1, 3), at_final(1), at_final(2), at_final(3)]
    for partner in partners:
        pl.semaphore_signal(barrier, inc=1, device_id=partner, device_id_type=MESH)
    pl.semaphore_wait(barrier, len(partners))

    def remote(src, dst, send, recv, target):
        return pltpu.make_async_remote_copy(
            src_ref=src, dst_ref=dst, send_sem=send, recv_sem=recv, device_id=target, device_id_type=MESH
        )

    def z_copy(kind, h):
        source, slot, hops = ROUTES[kind]
        return remote(
            kv.at[source, h], kv.at[slot, h], z_send.at[kind, h], z_recv.at[kind, h], z_places[hops]
        )

    def x_query(h):
        return remote(q_s.at[0, h], q_s.at[1, h], q_send.at[h], q_recv.at[h], across_x)

    def w_copy(k):
        return remote(w_hbm, w_all.at[y, my_rows], w_send.at[k], w_recv.at[k], at_owner(0, k))

    def w_share(k):
        place = w_all.at[quarters[-k % Y], my_rows]
        return remote(place, place, w_send.at[Y + k], w_recv.at[Y + k], other_core)

    def a_copy(kind, k, h):
        quarter = quarters[k]
        source, target = ((att, att_in), (part, part_in))[kind]
        sem = (kind, k, h)
        return remote(source.at[h, quarter], target.at[y, h], a_send.at[sem], a_recv.at[sem], at_owner(kind, k))

    def f_copy(k, part):
        piece = (xh + k // 2) % 2 * 2 + (c + k) % 2
        return remote(
            send_o.at[part, piece], recv_o.at[part, k], f_send.at[part, k], f_recv.at[part, k], at_final(k)
        )

    for h in range(HEADS_DEV):
        local_copy(0, h).wait()
        local_copy(1, h).wait()
        z_copy(CHAIN, h).start()
    for h in range(HEADS_DEV):
        z_copy(OPPOSITE, h).start()
    for h in range(HEADS_DEV):
        local_copy(2, h).wait()

        @pl.when(helped)
        def _():
            x_query(h).start()

    for k in range(1, Y):
        w_copy(k).start()
    w_local.wait()
    w_share(0).start()

    group = y * 2 + xh
    scaling = LOG2E / math.sqrt(HD)
    column = lax.broadcasted_iota(jnp.int32, (1, TOK), 1) // TILE

    ones = jnp.ones((TOK, HD), BF)

    def attend(owner, h, slot, far_frame, far_row, first=False):
        head_id = group * HEADS_DEV + h
        allowed = (far_frame <= windows[0, head_id]) & (far_row <= windows[1, head_id])
        same = jnp.where(allowed, 0.0, NEGATIVE)
        other = jnp.where(allowed & (windows[2, head_id] >= 1), 0.0, NEGATIVE)
        keys = kv[slot, h, 0]
        values = jnp.concatenate([kv[slot, h, 1], ones], axis=1)
        for half in range(2):
            rows = pl.ds(half * TILE, TILE)
            bias = jnp.where(column == half, same, other)
            scores = lax.dot_general(
                q_s[owner, h, rows], keys, (((1,), (1,)), ((), ())), preferred_element_type=F32
            )
            scores = scores * scaling + bias
            peak = jnp.max(scores, axis=1, keepdims=True)
            if not first:
                before = m_s[owner, h, rows, :1]
                peak = jnp.maximum(peak, before)
            weights = jnp.exp2(scores - peak)
            mixed = jnp.dot(weights.astype(BF), values, preferred_element_type=F32)
            mixed, total = mixed[:, :HD], mixed[:, HD:]
            if not first:
                fade = jnp.exp2(before - peak)
                total += fade * l_s[owner, h, rows]
                mixed += fade * acc_s[owner, h, rows]
            m_s[owner, h, rows] = jnp.broadcast_to(peak, (TILE, HD))
            l_s[owner, h, rows] = total
            acc_s[owner, h, rows] = mixed

    def in_grid(r):
        return (r >= 0) & (r < ROW_TILES)

    ahead, behind = in_grid(row + step), in_grid(row - step)

    def each_head(body):
        def run(h, carry):
            body(h)
            return carry

        lax.fori_loop(0, HEADS_DEV, run, 0)

    def hand_on(h):
        z_copy(CHAIN, h).wait_recv()
        z_copy(LEAP, h).start()

    def near(h):
        attend(0, h, 0, 0, 0, first=True)

        @pl.when(behind)
        def _():
            attend(0, h, 2, 0, 1)

    def near_opposite(h):
        z_copy(OPPOSITE, h).wait_recv()

        @pl.when(ahead)
        def _():
            attend(0, h, 1, 0, 1)

    def leap(h):
        z_copy(LEAP, h).wait_recv()
        z_copy(FAR, h).start()

    def far(h):
        z_copy(FAR, h).wait_recv()
        z_copy(FAR_SAME, h).start()

        @pl.when(helps)
        def _():
            x_query(h).wait_recv()
            m_s[1, h] = jnp.full((TOK, HD), NEGATIVE, F32)
            l_s[1, h] = jnp.zeros((TOK, HD), F32)
            acc_s[1, h] = jnp.zeros((TOK, HD), F32)

        @pl.when(ahead)
        def _():
            attend(0, h, 4, 1, 1)

        @pl.when(ahead & helps)
        def _():
            attend(1, h, 4, 1, 1)

    def far_same(h):
        z_copy(FAR_SAME, h).wait_recv()
        z_copy(FAR_LAST, h).start()
        attend(0, h, 5, 1, 0)

        @pl.when(helps)
        def _():
            attend(1, h, 5, 1, 0)

    blank = jnp.zeros((BLOCK - QUARTER, HD), BF)
    mask = lax.broadcasted_iota(jnp.int32, (QUARTER, HD), 0) == lax.broadcasted_iota(jnp.int32, (QUARTER, HD), 1)

    def close(target, owner, h):
        mixed = (acc_s[owner, h] / l_s[owner, h]).astype(BF)
        for quarter in range(Y):
            target[h, quarter, :QUARTER] = mixed[quarter * QUARTER : (quarter + 1) * QUARTER]

    def close_lse(target, owner, h):
        lse = m_s[owner, h] + jnp.log2(l_s[owner, h])
        place = lax.broadcasted_iota(jnp.int32, (BLOCK - QUARTER, HD), 0)
        for quarter in range(Y):
            rows = lse[quarter * QUARTER : (quarter + 1) * QUARTER]
            line = jnp.sum(jnp.where(mask, rows, 0.0), axis=0, keepdims=True)
            high = line.astype(BF).astype(F32)
            middle = (line - high).astype(BF).astype(F32)
            low = line - high - middle
            lines = jnp.where(place == 0, high, jnp.where(place == 1, middle, jnp.where(place == 2, low, 0.0)))
            target[h, quarter, QUARTER:] = lines.astype(BF)

    def far_last(h):
        z_copy(FAR_LAST, h).wait_recv()

        @pl.when(helps)
        def _():
            @pl.when(behind)
            def _():
                attend(1, h, 6, 1, 1)

            close(part, 1, h)
            close_lse(part, 1, h)
            for k in (2, 1, 3, 0):
                a_copy(PARTIAL, k, h).start()
            for quarter in range(Y):
                att[h, quarter, QUARTER:] = blank

        @pl.when(behind)
        def _():
            attend(0, h, 6, 1, 1)

        close(att, 0, h)

        @pl.when(helped)
        def _():
            close_lse(att, 0, h)

        for k in (2, 1, 3):
            a_copy(ATT, k, h).start()
        att_in[y, h] = att[h, y]

    def merged(own, other):
        def lse(block):
            lines = block[QUARTER:].astype(F32)
            return lines[0:1] + lines[1:2] + lines[2:3]

        first, second = lse(own), lse(other)
        peak = jnp.maximum(first, second)
        first, second = jnp.exp2(first - peak), jnp.exp2(second - peak)
        total = first + second
        shares = []
        for share in (first / total, second / total):
            high = share.astype(BF).astype(F32)
            shares += [jnp.where(mask, line, 0.0).astype(BF) for line in (high, share - high)]
        pad = jnp.zeros((HD - BLOCK, HD), BF)
        both_results = jnp.concatenate([own, pad, own, pad, other, pad, other, pad], axis=0)
        return jnp.dot(jnp.concatenate(shares, axis=1), both_results, preferred_element_type=F32).astype(BF)

    each_head(hand_on)
    each_head(near)
    each_head(near_opposite)
    each_head(leap)
    each_head(far)
    each_head(far_same)
    for k in range(1, Y):
        w_copy(k).wait_recv()
        w_share(k).start()
    each_head(far_last)

    for k in range(Y):
        w_share(k).wait_recv()
    last = HEADS_DEV - 1

    def arrived(h):
        for k in range(1, Y):
            a_copy(ATT, k, h).wait_recv()

        @pl.when(helped)
        def _():
            for k in range(Y):
                a_copy(PARTIAL, k, h).wait_recv()
            for s in range(Y):
                att_in[s, h, :QUARTER] = merged(att_in[s, h], part_in[s, h])

    def project(h, cols):
        rows = pl.ds(pl.multiple_of(h * HD, HD), HD)
        total = jnp.zeros((QUARTER, PART), F32)
        for s in range(Y):
            total += jnp.dot(
                att_in[s, h, :QUARTER], w_all[s, rows, cols], preferred_element_type=F32
            )
        return total

    for h in range(last):
        arrived(h)
        for part_index in range(PARTS):
            cols = pl.ds(part_index * PART, PART)
            if h == 0:
                acc_o[:, cols] = project(h, cols)
            else:
                acc_o[:, cols] += project(h, cols)
    arrived(last)
    for part_index in range(PARTS):
        cols = pl.ds(part_index * PART, PART)
        total = (acc_o[:, cols] + project(last, cols)).astype(BF)
        for piece in range(4):
            mine = total[piece * OWN : (piece + 1) * OWN]
            send_o[part_index, piece, :OWN] = mine[:, : PART // 2]
            send_o[part_index, piece, OWN:] = mine[:, PART // 2 :]
        for k in (2, 3, 1):
            f_copy(k, part_index).start()

    def sent(h):
        for kind in range(len(ROUTES)):
            z_copy(kind, h).wait_send()

        @pl.when(helps)
        def _():
            for k in range(Y):
                a_copy(PARTIAL, k, h).wait_send()

        @pl.when(helped)
        def _():
            x_query(h).wait_send()

        for k in range(1, Y):
            a_copy(ATT, k, h).wait_send()

    each_head(sent)
    for k in range(1, Y):
        w_copy(k).wait_send()
    for k in range(Y):
        w_share(k).wait_send()

    own = xh * 2 + c
    for part_index in range(PARTS):
        for k in range(1, 4):
            f_copy(k, part_index).wait_recv()
        mine = send_o[part_index, own].astype(F32) + recv_o[part_index, 2].astype(F32)
        others = recv_o[part_index, 1].astype(F32) + recv_o[part_index, 3].astype(F32)
        mine, others = mine.astype(BF), others.astype(BF)
        for side in range(2):
            cols = pl.ds(part_index * PART + side * PART // 2, PART // 2)
            rows = slice(side * OWN, (side + 1) * OWN)
            out_ref[0, :, cols] = jnp.where(c == 0, mine[rows], others[rows])
            out_ref[1, :, cols] = jnp.where(c == 0, others[rows], mine[rows])

    for part_index in range(PARTS):
        for k in range(1, 4):
            f_copy(k, part_index).wait_send()


def local(query_rows, key_rows, value_rows, windows, out_weight):
    dma = pltpu.SemaphoreType.DMA
    anywhere = pl.BlockSpec(memory_space=pl.ANY)
    return pl.pallas_call(
        kernel,
        out_shape=jax.ShapeDtypeStruct((SEEDS, OWN, D), BF),
        in_specs=[anywhere] * 3 + [pl.BlockSpec(memory_space=pltpu.SMEM), anywhere],
        out_specs=pl.BlockSpec(memory_space=pltpu.VMEM),
        scratch_shapes=[
            pltpu.VMEM((SLOTS, HEADS_DEV, 2, TOK, HD), BF),
            pltpu.VMEM((2, HEADS_DEV, TOK, HD), BF),
            pltpu.VMEM((Y, 2 * W_ROWS, D), BF),
            pltpu.VMEM((2, HEADS_DEV, TOK, HD), F32),
            pltpu.VMEM((2, HEADS_DEV, TOK, HD), F32),
            pltpu.VMEM((2, HEADS_DEV, TOK, HD), F32),
            pltpu.VMEM((HEADS_DEV, Y, BLOCK, HD), BF),
            pltpu.VMEM((HEADS_DEV, Y, BLOCK, HD), BF),
            pltpu.VMEM((Y, HEADS_DEV, BLOCK, HD), BF),
            pltpu.VMEM((Y, HEADS_DEV, BLOCK, HD), BF),
            pltpu.VMEM((QUARTER, D), F32),
            pltpu.VMEM((PARTS, 4, 2 * OWN, PART // 2), BF),
            pltpu.VMEM((PARTS, 4, 2 * OWN, PART // 2), BF),
            dma((4, HEADS_DEV)),
            dma((len(ROUTES), HEADS_DEV)),
            dma((len(ROUTES), HEADS_DEV)),
            dma((HEADS_DEV,)),
            dma((HEADS_DEV,)),
            dma((2, Y, HEADS_DEV)),
            dma((2, Y, HEADS_DEV)),
            dma((2 * Y,)),
            dma((2 * Y,)),
            dma((PARTS, 4)),
            dma((PARTS, 4)),
        ],
        compiler_params=pltpu.CompilerParams(
            collective_id=0, has_side_effects=True, vmem_limit_bytes=VMEM
        ),
        cost_estimate=pl.CostEstimate(
            flops=2 * (2 * HEADS_DEV * TOK * 9 * TOK * HD + TOK * HEADS_DEV * HD * D),
            bytes_accessed=4 << 20,
            transcendentals=HEADS_DEV * TOK * 9 * TOK,
        ),
    )(query_rows, key_rows, value_rows, windows.T, out_weight)


def solution(mesh):
    placed = (P("frame", "head"), P("frame", "head"), P("frame", "head"), P(), P("head", None))
    return jax.shard_map(
        local,
        mesh=mesh,
        in_specs=placed,
        out_specs=P(None, ("frame", "head"), None),
        check_vma=False,
    )
```

```python
import math

import jax
import jax.numpy as jnp
from jax import lax
from jax.experimental import pallas as pl
from jax.experimental.pallas import tpu as pltpu
from jax.sharding import PartitionSpec as P

HD = 128
SEEDS = 2
FRAME_TILES = 4
NEGATIVE = -1e30
VMEM = 56164352
MESH = pl.DeviceIdType.MESH
BF = jnp.bfloat16
F32 = jnp.float32

Z, Y = 16, 4
ROW_TILES = 8
HEADS_DEV = 3
TOK = 384
TILE = 192
D = 3072
W_ROWS = 192
OWN = 24
QUARTER = 96

CHAIN, OPPOSITE, LEAP, LEAP_ON, FAR, FAR_SAME, FAR_LAST = range(7)
ROUTES = ((0, 2, 1), (0, 1, -1), (2, 3, 2), (3, 4, 2), (4, 5, 2), (5, 6, 1), (6, 7, 1))
SLOTS = 8
BLOCK = 112
PARTS = 2
PART = D // PARTS
LOG2E = math.log2(math.e)
ATT, PARTIAL = range(2)


def kernel(q_hbm, k_hbm, v_hbm, windows_hbm, w_hbm, out_ref, *scratch):
    (kv, q_s, w_all, m_s, l_s, acc_s, att, part, att_in, part_in, acc_o, send_o, recv_o) = scratch[:13]
    (local_sem, z_send, z_recv, q_send, q_recv, a_send, a_recv, w_send, w_recv, f_send, f_recv) = scratch[13:-1]
    windows = scratch[-1]

    frame = lax.axis_index("frame")
    head = lax.axis_index("head")
    xl, z = frame // Z, frame % Z
    y, xh, c = head // 4, (head // 2) % 2, head % 2
    row = z % ROW_TILES
    upper = z // ROW_TILES
    step = 2 * c - 1
    helps = upper == xl
    helped = upper != xl

    def z_place(distance):
        return (xl * Z + (z + distance + Z) % Z, head)

    z_places = {hops: z_place(hops * step) for hops in (-2, -1, 1, 2)}

    quarters = [(y + k) % Y for k in range(Y)]
    owners = [[((xl + a) % 2 * Z + z, quarter * 4 + xh * 2 + c) for quarter in quarters] for a in range(2)]

    def at_owner(across, k):
        return owners[across][k]

    across_x = ((1 - xl) * Z + z, head)
    other_core = (frame, y * 4 + xh * 2 + 1 - c)

    finals = [(frame, y * 4 + (xh + k // 2) % 2 * 2 + (c + k) % 2) for k in range(4)]

    def at_final(k):
        return finals[k]

    def local_copy(i, h):
        cols = pl.ds(pl.multiple_of(h * HD, HD), HD)
        source = (k_hbm, v_hbm, q_hbm)[i].at[:, cols]
        target = q_s.at[0, h] if i == 2 else kv.at[0, h, i]
        return pltpu.make_async_copy(source, target, local_sem.at[i, h])

    my_rows = pl.ds(pl.multiple_of(c * W_ROWS, W_ROWS), W_ROWS)
    w_local = pltpu.make_async_copy(w_hbm, w_all.at[y, my_rows], local_sem.at[3, 0])
    windows_copy = pltpu.make_async_copy(windows_hbm, windows, local_sem.at[3, 1])
    windows_copy.start()
    for i in range(3):
        for h in range(HEADS_DEV):
            local_copy(i, h).start()
    w_local.start()

    barrier = pltpu.get_barrier_semaphore()
    partners = [z_places[1], z_places[-1], z_places[2], z_places[-2], across_x]
    partners += [at_owner(0, 1), at_owner(0, 2), at_owner(0, 3), at_owner(1, 1), at_owner(1, 2), at_owner(1, 3), at_final(1), at_final(2), at_final(3)]
    for partner in partners:
        pl.semaphore_signal(barrier, inc=1, device_id=partner, device_id_type=MESH)
    pl.semaphore_wait(barrier, len(partners))

    def remote(src, dst, send, recv, target):
        return pltpu.make_async_remote_copy(
            src_ref=src, dst_ref=dst, send_sem=send, recv_sem=recv, device_id=target, device_id_type=MESH
        )

    def z_copy(kind, h):
        source, slot, hops = ROUTES[kind]
        return remote(
            kv.at[source, h], kv.at[slot, h], z_send.at[kind, h], z_recv.at[kind, h], z_places[hops]
        )

    def x_query(h):
        return remote(q_s.at[0, h], q_s.at[1, h], q_send.at[h], q_recv.at[h], across_x)

    def w_copy(k):
        return remote(w_hbm, w_all.at[y, my_rows], w_send.at[k], w_recv.at[k], at_owner(0, k))

    def w_share(k):
        place = w_all.at[quarters[-k % Y], my_rows]
        return remote(place, place, w_send.at[Y + k], w_recv.at[Y + k], other_core)

    def a_copy(kind, k, h):
        quarter = quarters[k]
        source, target = ((att, att_in), (part, part_in))[kind]
        sem = (kind, k, h)
        return remote(source.at[h, quarter], target.at[y, h], a_send.at[sem], a_recv.at[sem], at_owner(kind, k))

    def f_copy(k, part):
        piece = (xh + k // 2) % 2 * 2 + (c + k) % 2
        return remote(
            send_o.at[part, piece], recv_o.at[part, k], f_send.at[part, k], f_recv.at[part, k], at_final(k)
        )

    for h in range(HEADS_DEV):
        local_copy(0, h).wait()
        local_copy(1, h).wait()
        z_copy(CHAIN, h).start()
    for h in range(HEADS_DEV):
        z_copy(OPPOSITE, h).start()
    for h in range(HEADS_DEV):
        local_copy(2, h).wait()

        @pl.when(helped)
        def _():
            x_query(h).start()

    for k in range(1, Y):
        w_copy(k).start()
    w_local.wait()
    w_share(0).start()

    windows_copy.wait()
    group = y * 2 + xh
    scaling = LOG2E / math.sqrt(HD)
    column = lax.broadcasted_iota(jnp.int32, (1, TOK), 1) // TILE

    ones = jnp.ones((TOK, HD), BF)

    def attend(owner, h, slot, far_frame, far_row, first=False):
        head_id = group * HEADS_DEV + h
        allowed = (far_frame <= windows[0, head_id]) & (far_row <= windows[1, head_id])
        same = jnp.where(allowed, 0.0, NEGATIVE)
        other = jnp.where(allowed & (windows[2, head_id] >= 1), 0.0, NEGATIVE)
        keys = kv[slot, h, 0]
        values = jnp.concatenate([kv[slot, h, 1], ones], axis=1)
        for half in range(2):
            rows = pl.ds(half * TILE, TILE)
            bias = jnp.where(column == half, same, other)
            scores = lax.dot_general(
                q_s[owner, h, rows], keys, (((1,), (1,)), ((), ())), preferred_element_type=F32
            )
            scores = scores * scaling + bias
            peak = jnp.max(scores, axis=1, keepdims=True)
            if not first:
                before = m_s[owner, h, rows, :1]
                peak = jnp.maximum(peak, before)
            weights = jnp.exp2(scores - peak)
            mixed = jnp.dot(weights.astype(BF), values, preferred_element_type=F32)
            mixed, total = mixed[:, :HD], mixed[:, HD:]
            if not first:
                fade = jnp.exp2(before - peak)
                total += fade * l_s[owner, h, rows]
                mixed += fade * acc_s[owner, h, rows]
            m_s[owner, h, rows] = jnp.broadcast_to(peak, (TILE, HD))
            l_s[owner, h, rows] = total
            acc_s[owner, h, rows] = mixed

    def in_grid(r):
        return (r >= 0) & (r < ROW_TILES)

    ahead, behind = in_grid(row + step), in_grid(row - step)

    def each_head(body):
        def run(h, carry):
            body(h)
            return carry

        lax.fori_loop(0, HEADS_DEV, run, 0)

    def hand_on(h):
        z_copy(CHAIN, h).wait_recv()
        z_copy(LEAP, h).start()

    def near(h):
        attend(0, h, 0, 0, 0, first=True)

        @pl.when(behind)
        def _():
            attend(0, h, 2, 0, 1)

    def near_opposite(h):
        z_copy(OPPOSITE, h).wait_recv()

        @pl.when(ahead)
        def _():
            attend(0, h, 1, 0, 1)

    def leap(h):
        z_copy(LEAP, h).wait_recv()
        z_copy(LEAP_ON, h).start()

    def leap_on(h):
        z_copy(LEAP_ON, h).wait_recv()
        z_copy(FAR, h).start()

    def far(h):
        z_copy(FAR, h).wait_recv()
        z_copy(FAR_SAME, h).start()

        @pl.when(helps)
        def _():
            x_query(h).wait_recv()
            m_s[1, h] = jnp.full((TOK, HD), NEGATIVE, F32)
            l_s[1, h] = jnp.zeros((TOK, HD), F32)
            acc_s[1, h] = jnp.zeros((TOK, HD), F32)

        @pl.when(ahead)
        def _():
            attend(0, h, 5, 1, 1)

        @pl.when(ahead & helps)
        def _():
            attend(1, h, 5, 1, 1)

    def far_same(h):
        z_copy(FAR_SAME, h).wait_recv()
        z_copy(FAR_LAST, h).start()
        attend(0, h, 6, 1, 0)

        @pl.when(helps)
        def _():
            attend(1, h, 6, 1, 0)

    blank = jnp.zeros((BLOCK - QUARTER, HD), BF)
    mask = lax.broadcasted_iota(jnp.int32, (QUARTER, HD), 0) == lax.broadcasted_iota(jnp.int32, (QUARTER, HD), 1)

    def close(target, owner, h):
        mixed = (acc_s[owner, h] / l_s[owner, h]).astype(BF)
        for quarter in range(Y):
            target[h, quarter, :QUARTER] = mixed[quarter * QUARTER : (quarter + 1) * QUARTER]

    def close_lse(target, owner, h):
        lse = m_s[owner, h] + jnp.log2(l_s[owner, h])
        place = lax.broadcasted_iota(jnp.int32, (BLOCK - QUARTER, HD), 0)
        for quarter in range(Y):
            rows = lse[quarter * QUARTER : (quarter + 1) * QUARTER]
            line = jnp.sum(jnp.where(mask, rows, 0.0), axis=0, keepdims=True)
            high = line.astype(BF).astype(F32)
            middle = (line - high).astype(BF).astype(F32)
            low = line - high - middle
            lines = jnp.where(place == 0, high, jnp.where(place == 1, middle, jnp.where(place == 2, low, 0.0)))
            target[h, quarter, QUARTER:] = lines.astype(BF)

    def far_last(h):
        z_copy(FAR_LAST, h).wait_recv()

        @pl.when(helps)
        def _():
            @pl.when(behind)
            def _():
                attend(1, h, 7, 1, 1)

            close(part, 1, h)
            close_lse(part, 1, h)
            for k in (2, 1, 3, 0):
                a_copy(PARTIAL, k, h).start()
            for quarter in range(Y):
                att[h, quarter, QUARTER:] = blank

        @pl.when(behind)
        def _():
            attend(0, h, 7, 1, 1)

        close(att, 0, h)

        @pl.when(helped)
        def _():
            close_lse(att, 0, h)

        for k in (2, 1, 3):
            a_copy(ATT, k, h).start()
        att_in[y, h] = att[h, y]

    def merged(own, other):
        def lse(block):
            lines = block[QUARTER:].astype(F32)
            return lines[0:1] + lines[1:2] + lines[2:3]

        first, second = lse(own), lse(other)
        peak = jnp.maximum(first, second)
        first, second = jnp.exp2(first - peak), jnp.exp2(second - peak)
        total = first + second
        shares = []
        for share in (first / total, second / total):
            high = share.astype(BF).astype(F32)
            shares += [jnp.where(mask, line, 0.0).astype(BF) for line in (high, share - high)]
        pad = jnp.zeros((HD - BLOCK, HD), BF)
        both_results = jnp.concatenate([own, pad, own, pad, other, pad, other, pad], axis=0)
        return jnp.dot(jnp.concatenate(shares, axis=1), both_results, preferred_element_type=F32).astype(BF)

    each_head(hand_on)
    each_head(near)
    each_head(near_opposite)
    each_head(leap)
    each_head(leap_on)
    each_head(far)
    each_head(far_same)
    for k in range(1, Y):
        w_copy(k).wait_recv()
        w_share(k).start()
    each_head(far_last)

    for k in range(Y):
        w_share(k).wait_recv()
    last = HEADS_DEV - 1

    def arrived(h):
        for k in range(1, Y):
            a_copy(ATT, k, h).wait_recv()

        @pl.when(helped)
        def _():
            for k in range(Y):
                a_copy(PARTIAL, k, h).wait_recv()
            for s in range(Y):
                att_in[s, h, :QUARTER] = merged(att_in[s, h], part_in[s, h])

    def project(h, cols):
        rows = pl.ds(pl.multiple_of(h * HD, HD), HD)
        total = jnp.zeros((QUARTER, PART), F32)
        for s in range(Y):
            total += jnp.dot(
                att_in[s, h, :QUARTER], w_all[s, rows, cols], preferred_element_type=F32
            )
        return total

    for h in range(last):
        arrived(h)
        for part_index in range(PARTS):
            cols = pl.ds(part_index * PART, PART)
            if h == 0:
                acc_o[:, cols] = project(h, cols)
            else:
                acc_o[:, cols] += project(h, cols)
    arrived(last)
    for part_index in range(PARTS):
        cols = pl.ds(part_index * PART, PART)
        total = (acc_o[:, cols] + project(last, cols)).astype(BF)
        for piece in range(4):
            mine = total[piece * OWN : (piece + 1) * OWN]
            send_o[part_index, piece, :OWN] = mine[:, : PART // 2]
            send_o[part_index, piece, OWN:] = mine[:, PART // 2 :]
        for k in (2, 3, 1):
            f_copy(k, part_index).start()

    def sent(h):
        for kind in range(len(ROUTES)):
            z_copy(kind, h).wait_send()

        @pl.when(helps)
        def _():
            for k in range(Y):
                a_copy(PARTIAL, k, h).wait_send()

        @pl.when(helped)
        def _():
            x_query(h).wait_send()

        for k in range(1, Y):
            a_copy(ATT, k, h).wait_send()

    each_head(sent)
    for k in range(1, Y):
        w_copy(k).wait_send()
    for k in range(Y):
        w_share(k).wait_send()

    own = xh * 2 + c
    for part_index in range(PARTS):
        for k in range(1, 4):
            f_copy(k, part_index).wait_recv()
        mine = send_o[part_index, own].astype(F32) + recv_o[part_index, 2].astype(F32)
        others = recv_o[part_index, 1].astype(F32) + recv_o[part_index, 3].astype(F32)
        mine, others = mine.astype(BF), others.astype(BF)
        for side in range(2):
            cols = pl.ds(part_index * PART + side * PART // 2, PART // 2)
            rows = slice(side * OWN, (side + 1) * OWN)
            out_ref[0, :, cols] = jnp.where(c == 0, mine[rows], others[rows])
            out_ref[1, :, cols] = jnp.where(c == 0, others[rows], mine[rows])

    for part_index in range(PARTS):
        for k in range(1, 4):
            f_copy(k, part_index).wait_send()


def local(query_rows, key_rows, value_rows, windows, out_weight):
    dma = pltpu.SemaphoreType.DMA
    anywhere = pl.BlockSpec(memory_space=pl.ANY)
    return pl.pallas_call(
        kernel,
        out_shape=jax.ShapeDtypeStruct((SEEDS, OWN, D), BF),
        in_specs=[anywhere] * 5,
        out_specs=pl.BlockSpec(memory_space=pltpu.VMEM),
        scratch_shapes=[
            pltpu.VMEM((SLOTS, HEADS_DEV, 2, TOK, HD), BF),
            pltpu.VMEM((2, HEADS_DEV, TOK, HD), BF),
            pltpu.VMEM((Y, 2 * W_ROWS, D), BF),
            pltpu.VMEM((2, HEADS_DEV, TOK, HD), F32),
            pltpu.VMEM((2, HEADS_DEV, TOK, HD), F32),
            pltpu.VMEM((2, HEADS_DEV, TOK, HD), F32),
            pltpu.VMEM((HEADS_DEV, Y, BLOCK, HD), BF),
            pltpu.VMEM((HEADS_DEV, Y, BLOCK, HD), BF),
            pltpu.VMEM((Y, HEADS_DEV, BLOCK, HD), BF),
            pltpu.VMEM((Y, HEADS_DEV, BLOCK, HD), BF),
            pltpu.VMEM((QUARTER, D), F32),
            pltpu.VMEM((PARTS, 4, 2 * OWN, PART // 2), BF),
            pltpu.VMEM((PARTS, 4, 2 * OWN, PART // 2), BF),
            dma((4, HEADS_DEV)),
            dma((len(ROUTES), HEADS_DEV)),
            dma((len(ROUTES), HEADS_DEV)),
            dma((HEADS_DEV,)),
            dma((HEADS_DEV,)),
            dma((2, Y, HEADS_DEV)),
            dma((2, Y, HEADS_DEV)),
            dma((2 * Y,)),
            dma((2 * Y,)),
            dma((PARTS, 4)),
            dma((PARTS, 4)),
            pltpu.SMEM((3, 24), jnp.int32),
        ],
        compiler_params=pltpu.CompilerParams(
            collective_id=0, has_side_effects=True, vmem_limit_bytes=VMEM
        ),
        cost_estimate=pl.CostEstimate(
            flops=2 * (2 * HEADS_DEV * TOK * 9 * TOK * HD + TOK * HEADS_DEV * HD * D),
            bytes_accessed=4 << 20,
            transcendentals=HEADS_DEV * TOK * 9 * TOK,
        ),
    )(query_rows, key_rows, value_rows, windows.T, out_weight)


def solution(mesh):
    placed = (P("frame", "head"), P("frame", "head"), P("frame", "head"), P(), P("head", None))
    return jax.shard_map(
        local,
        mesh=mesh,
        in_specs=placed,
        out_specs=P(None, ("frame", "head"), None),
        check_vma=False,
    )
```

```python
import math

import jax
import jax.numpy as jnp
from jax import lax
from jax.experimental import pallas as pl
from jax.experimental.pallas import tpu as pltpu
from jax.sharding import PartitionSpec as P

HD = 128
SEEDS = 2
FRAME_TILES = 4
NEGATIVE = -1e30
VMEM = 56164352
MESH = pl.DeviceIdType.MESH
BF = jnp.bfloat16
F32 = jnp.float32

Z, Y = 16, 4
ROW_TILES = 8
HEADS_DEV = 3
TOK = 384
TILE = 192
D = 3072
W_ROWS = 192
OWN = 24
QUARTER = 96

CHAIN, OPPOSITE, LEAP, LEAP_ON, FAR, FAR_SAME, FAR_LAST = range(7)
ROUTES = ((0, 2, 1), (0, 1, -1), (2, 3, 2), (3, 4, 2), (4, 5, 2), (5, 6, 1), (6, 7, 1))
SLOTS = 8
BLOCK = 112
PARTS = 2
PART = D // PARTS
LOG2E = math.log2(math.e)
ATT, PARTIAL = range(2)


def kernel(q_hbm, k_hbm, v_hbm, windows_hbm, w_hbm, out_ref, *scratch):
    (kv, q_s, w_all, m_s, l_s, acc_s, att, part, att_in, part_in, acc_o, send_o, recv_o) = scratch[:13]
    (local_sem, z_send, z_recv, q_send, q_recv, a_send, a_recv, w_send, w_recv, f_send, f_recv) = scratch[13:-1]
    windows = scratch[-1]

    frame = lax.axis_index("frame")
    head = lax.axis_index("head")
    xl, z = frame // Z, frame % Z
    y, xh, c = head // 4, (head // 2) % 2, head % 2
    row = z % ROW_TILES
    upper = z // ROW_TILES
    step = 2 * c - 1
    helps = upper == xl
    helped = upper != xl

    def z_place(distance):
        return (xl * Z + (z + distance + Z) % Z, head)

    z_places = {hops: z_place(hops * step) for hops in (-2, -1, 1, 2)}

    quarters = [(y + k) % Y for k in range(Y)]
    owners = [[((xl + a) % 2 * Z + z, quarter * 4 + xh * 2 + c) for quarter in quarters] for a in range(2)]

    def at_owner(across, k):
        return owners[across][k]

    across_x = ((1 - xl) * Z + z, head)
    other_core = (frame, y * 4 + xh * 2 + 1 - c)

    finals = [(frame, y * 4 + (xh + k // 2) % 2 * 2 + (c + k) % 2) for k in range(4)]

    def at_final(k):
        return finals[k]

    def local_copy(i, h):
        cols = pl.ds(pl.multiple_of(h * HD, HD), HD)
        source = (k_hbm, v_hbm, q_hbm)[i].at[:, cols]
        target = q_s.at[0, h] if i == 2 else kv.at[0, h, i]
        return pltpu.make_async_copy(source, target, local_sem.at[i, h])

    my_rows = pl.ds(pl.multiple_of(c * W_ROWS, W_ROWS), W_ROWS)
    w_local = pltpu.make_async_copy(w_hbm, w_all.at[y, my_rows], local_sem.at[3, 0])

    barrier = pltpu.get_barrier_semaphore()
    partners = [z_places[1], z_places[-1], z_places[2], z_places[-2], across_x]
    partners += [at_owner(0, 1), at_owner(0, 2), at_owner(0, 3), at_owner(1, 1), at_owner(1, 2), at_owner(1, 3), at_final(1), at_final(2), at_final(3)]
    for partner in partners:
        pl.semaphore_signal(barrier, inc=1, device_id=partner, device_id_type=MESH)

    windows_copy = pltpu.make_async_copy(windows_hbm, windows, local_sem.at[3, 1])
    windows_copy.start()
    for i in range(3):
        for h in range(HEADS_DEV):
            local_copy(i, h).start()
    w_local.start()

    pl.semaphore_wait(barrier, len(partners))

    def remote(src, dst, send, recv, target):
        return pltpu.make_async_remote_copy(
            src_ref=src, dst_ref=dst, send_sem=send, recv_sem=recv, device_id=target, device_id_type=MESH
        )

    def z_copy(kind, h):
        source, slot, hops = ROUTES[kind]
        return remote(
            kv.at[source, h], kv.at[slot, h], z_send.at[kind, h], z_recv.at[kind, h], z_places[hops]
        )

    def x_query(h):
        return remote(q_s.at[0, h], q_s.at[1, h], q_send.at[h], q_recv.at[h], across_x)

    def w_copy(k):
        return remote(w_hbm, w_all.at[y, my_rows], w_send.at[k], w_recv.at[k], at_owner(0, k))

    def w_share(k):
        place = w_all.at[quarters[-k % Y], my_rows]
        return remote(place, place, w_send.at[Y + k], w_recv.at[Y + k], other_core)

    def a_copy(kind, k, h):
        quarter = quarters[k]
        source, target = ((att, att_in), (part, part_in))[kind]
        sem = (kind, k, h)
        return remote(source.at[h, quarter], target.at[y, h], a_send.at[sem], a_recv.at[sem], at_owner(kind, k))

    def f_copy(k, part):
        piece = (xh + k // 2) % 2 * 2 + (c + k) % 2
        return remote(
            send_o.at[part, piece], recv_o.at[part, k], f_send.at[part, k], f_recv.at[part, k], at_final(k)
        )

    for h in range(HEADS_DEV):
        local_copy(0, h).wait()
        local_copy(1, h).wait()
        z_copy(CHAIN, h).start()
    for h in range(HEADS_DEV):
        z_copy(OPPOSITE, h).start()
    for h in range(HEADS_DEV):
        local_copy(2, h).wait()

        @pl.when(helped)
        def _():
            x_query(h).start()

    for k in range(1, Y):
        w_copy(k).start()
    w_local.wait()
    w_share(0).start()

    windows_copy.wait()
    group = y * 2 + xh
    scaling = LOG2E / math.sqrt(HD)
    column = lax.broadcasted_iota(jnp.int32, (1, TOK), 1) // TILE

    ones = jnp.ones((TOK, HD), BF)

    def attend(owner, h, slot, far_frame, far_row, first=False):
        head_id = group * HEADS_DEV + h
        allowed = (far_frame <= windows[0, head_id]) & (far_row <= windows[1, head_id])
        same = jnp.where(allowed, 0.0, NEGATIVE)
        other = jnp.where(allowed & (windows[2, head_id] >= 1), 0.0, NEGATIVE)
        keys = kv[slot, h, 0]
        values = jnp.concatenate([kv[slot, h, 1], ones], axis=1)
        for half in range(2):
            rows = pl.ds(half * TILE, TILE)
            bias = jnp.where(column == half, same, other)
            scores = lax.dot_general(
                q_s[owner, h, rows], keys, (((1,), (1,)), ((), ())), preferred_element_type=F32
            )
            scores = scores * scaling + bias
            peak = jnp.max(scores, axis=1, keepdims=True)
            if not first:
                before = m_s[owner, h, rows, :1]
                peak = jnp.maximum(peak, before)
            weights = jnp.exp2(scores - peak)
            mixed = jnp.dot(weights.astype(BF), values, preferred_element_type=F32)
            mixed, total = mixed[:, :HD], mixed[:, HD:]
            if not first:
                fade = jnp.exp2(before - peak)
                total += fade * l_s[owner, h, rows]
                mixed += fade * acc_s[owner, h, rows]
            m_s[owner, h, rows] = jnp.broadcast_to(peak, (TILE, HD))
            l_s[owner, h, rows] = total
            acc_s[owner, h, rows] = mixed

    def in_grid(r):
        return (r >= 0) & (r < ROW_TILES)

    ahead, behind = in_grid(row + step), in_grid(row - step)

    def each_head(body):
        def run(h, carry):
            body(h)
            return carry

        lax.fori_loop(0, HEADS_DEV, run, 0)

    def hand_on(h):
        z_copy(CHAIN, h).wait_recv()
        z_copy(LEAP, h).start()

    def near(h):
        attend(0, h, 0, 0, 0, first=True)

        @pl.when(behind)
        def _():
            attend(0, h, 2, 0, 1)

    def near_opposite(h):
        z_copy(OPPOSITE, h).wait_recv()

        @pl.when(ahead)
        def _():
            attend(0, h, 1, 0, 1)

    def leap(h):
        z_copy(LEAP, h).wait_recv()
        z_copy(LEAP_ON, h).start()

    def leap_on(h):
        z_copy(LEAP_ON, h).wait_recv()
        z_copy(FAR, h).start()

    def far(h):
        z_copy(FAR, h).wait_recv()
        z_copy(FAR_SAME, h).start()

        @pl.when(helps)
        def _():
            x_query(h).wait_recv()
            m_s[1, h] = jnp.full((TOK, HD), NEGATIVE, F32)
            l_s[1, h] = jnp.zeros((TOK, HD), F32)
            acc_s[1, h] = jnp.zeros((TOK, HD), F32)

        @pl.when(ahead)
        def _():
            attend(0, h, 5, 1, 1)

        @pl.when(ahead & helps)
        def _():
            attend(1, h, 5, 1, 1)

    def far_same(h):
        z_copy(FAR_SAME, h).wait_recv()
        z_copy(FAR_LAST, h).start()
        attend(0, h, 6, 1, 0)

        @pl.when(helps)
        def _():
            attend(1, h, 6, 1, 0)

    blank = jnp.zeros((BLOCK - QUARTER, HD), BF)
    mask = lax.broadcasted_iota(jnp.int32, (QUARTER, HD), 0) == lax.broadcasted_iota(jnp.int32, (QUARTER, HD), 1)

    def close(target, owner, h):
        mixed = (acc_s[owner, h] / l_s[owner, h]).astype(BF)
        for quarter in range(Y):
            target[h, quarter, :QUARTER] = mixed[quarter * QUARTER : (quarter + 1) * QUARTER]

    def close_lse(target, owner, h):
        lse = m_s[owner, h] + jnp.log2(l_s[owner, h])
        place = lax.broadcasted_iota(jnp.int32, (BLOCK - QUARTER, HD), 0)
        for quarter in range(Y):
            rows = lse[quarter * QUARTER : (quarter + 1) * QUARTER]
            line = jnp.sum(jnp.where(mask, rows, 0.0), axis=0, keepdims=True)
            high = line.astype(BF).astype(F32)
            middle = (line - high).astype(BF).astype(F32)
            low = line - high - middle
            lines = jnp.where(place == 0, high, jnp.where(place == 1, middle, jnp.where(place == 2, low, 0.0)))
            target[h, quarter, QUARTER:] = lines.astype(BF)

    def far_last(h):
        z_copy(FAR_LAST, h).wait_recv()

        @pl.when(helps)
        def _():
            @pl.when(behind)
            def _():
                attend(1, h, 7, 1, 1)

            close(part, 1, h)
            close_lse(part, 1, h)
            for k in (2, 1, 3, 0):
                a_copy(PARTIAL, k, h).start()
            for quarter in range(Y):
                att[h, quarter, QUARTER:] = blank

        @pl.when(behind)
        def _():
            attend(0, h, 7, 1, 1)

        close(att, 0, h)

        @pl.when(helped)
        def _():
            close_lse(att, 0, h)

        for k in (2, 1, 3):
            a_copy(ATT, k, h).start()
        att_in[y, h] = att[h, y]

    def merged(own, other):
        def lse(block):
            lines = block[QUARTER:].astype(F32)
            return lines[0:1] + lines[1:2] + lines[2:3]

        first, second = lse(own), lse(other)
        peak = jnp.maximum(first, second)
        first, second = jnp.exp2(first - peak), jnp.exp2(second - peak)
        total = first + second
        shares = []
        for share in (first / total, second / total):
            high = share.astype(BF).astype(F32)
            shares += [jnp.where(mask, line, 0.0).astype(BF) for line in (high, share - high)]
        pad = jnp.zeros((HD - BLOCK, HD), BF)
        both_results = jnp.concatenate([own, pad, own, pad, other, pad, other, pad], axis=0)
        return jnp.dot(jnp.concatenate(shares, axis=1), both_results, preferred_element_type=F32).astype(BF)

    each_head(hand_on)
    each_head(near)
    each_head(near_opposite)
    each_head(leap)
    each_head(leap_on)
    each_head(far)
    each_head(far_same)
    for k in range(1, Y):
        w_copy(k).wait_recv()
        w_share(k).start()
    each_head(far_last)

    for k in range(Y):
        w_share(k).wait_recv()
    last = HEADS_DEV - 1

    def arrived(h):
        for k in range(1, Y):
            a_copy(ATT, k, h).wait_recv()

        @pl.when(helped)
        def _():
            for k in range(Y):
                a_copy(PARTIAL, k, h).wait_recv()
            for s in range(Y):
                att_in[s, h, :QUARTER] = merged(att_in[s, h], part_in[s, h])

    def project(h, cols):
        rows = pl.ds(pl.multiple_of(h * HD, HD), HD)
        total = jnp.zeros((QUARTER, PART), F32)
        for s in range(Y):
            total += jnp.dot(
                att_in[s, h, :QUARTER], w_all[s, rows, cols], preferred_element_type=F32
            )
        return total

    for h in range(last):
        arrived(h)
        for part_index in range(PARTS):
            cols = pl.ds(part_index * PART, PART)
            if h == 0:
                acc_o[:, cols] = project(h, cols)
            else:
                acc_o[:, cols] += project(h, cols)
    arrived(last)
    for part_index in range(PARTS):
        cols = pl.ds(part_index * PART, PART)
        total = (acc_o[:, cols] + project(last, cols)).astype(BF)
        for piece in range(4):
            mine = total[piece * OWN : (piece + 1) * OWN]
            send_o[part_index, piece, :OWN] = mine[:, : PART // 2]
            send_o[part_index, piece, OWN:] = mine[:, PART // 2 :]
        for k in (2, 3, 1):
            f_copy(k, part_index).start()

    def sent(h):
        for kind in range(len(ROUTES)):
            z_copy(kind, h).wait_send()

        @pl.when(helps)
        def _():
            for k in range(Y):
                a_copy(PARTIAL, k, h).wait_send()

        @pl.when(helped)
        def _():
            x_query(h).wait_send()

        for k in range(1, Y):
            a_copy(ATT, k, h).wait_send()

    each_head(sent)
    for k in range(1, Y):
        w_copy(k).wait_send()
    for k in range(Y):
        w_share(k).wait_send()

    own = xh * 2 + c
    for part_index in range(PARTS):
        for k in range(1, 4):
            f_copy(k, part_index).wait_recv()
        mine = send_o[part_index, own].astype(F32) + recv_o[part_index, 2].astype(F32)
        others = recv_o[part_index, 1].astype(F32) + recv_o[part_index, 3].astype(F32)
        mine, others = mine.astype(BF), others.astype(BF)
        for side in range(2):
            cols = pl.ds(part_index * PART + side * PART // 2, PART // 2)
            rows = slice(side * OWN, (side + 1) * OWN)
            out_ref[0, :, cols] = jnp.where(c == 0, mine[rows], others[rows])
            out_ref[1, :, cols] = jnp.where(c == 0, others[rows], mine[rows])

    for part_index in range(PARTS):
        for k in range(1, 4):
            f_copy(k, part_index).wait_send()


def local(query_rows, key_rows, value_rows, windows, out_weight):
    dma = pltpu.SemaphoreType.DMA
    anywhere = pl.BlockSpec(memory_space=pl.ANY)
    return pl.pallas_call(
        kernel,
        out_shape=jax.ShapeDtypeStruct((SEEDS, OWN, D), BF),
        in_specs=[anywhere] * 5,
        out_specs=pl.BlockSpec(memory_space=pltpu.VMEM),
        scratch_shapes=[
            pltpu.VMEM((SLOTS, HEADS_DEV, 2, TOK, HD), BF),
            pltpu.VMEM((2, HEADS_DEV, TOK, HD), BF),
            pltpu.VMEM((Y, 2 * W_ROWS, D), BF),
            pltpu.VMEM((2, HEADS_DEV, TOK, HD), F32),
            pltpu.VMEM((2, HEADS_DEV, TOK, HD), F32),
            pltpu.VMEM((2, HEADS_DEV, TOK, HD), F32),
            pltpu.VMEM((HEADS_DEV, Y, BLOCK, HD), BF),
            pltpu.VMEM((HEADS_DEV, Y, BLOCK, HD), BF),
            pltpu.VMEM((Y, HEADS_DEV, BLOCK, HD), BF),
            pltpu.VMEM((Y, HEADS_DEV, BLOCK, HD), BF),
            pltpu.VMEM((QUARTER, D), F32),
            pltpu.VMEM((PARTS, 4, 2 * OWN, PART // 2), BF),
            pltpu.VMEM((PARTS, 4, 2 * OWN, PART // 2), BF),
            dma((4, HEADS_DEV)),
            dma((len(ROUTES), HEADS_DEV)),
            dma((len(ROUTES), HEADS_DEV)),
            dma((HEADS_DEV,)),
            dma((HEADS_DEV,)),
            dma((2, Y, HEADS_DEV)),
            dma((2, Y, HEADS_DEV)),
            dma((2 * Y,)),
            dma((2 * Y,)),
            dma((PARTS, 4)),
            dma((PARTS, 4)),
            pltpu.SMEM((3, 24), jnp.int32),
        ],
        compiler_params=pltpu.CompilerParams(
            collective_id=0, has_side_effects=True, vmem_limit_bytes=VMEM
        ),
        cost_estimate=pl.CostEstimate(
            flops=2 * (2 * HEADS_DEV * TOK * 9 * TOK * HD + TOK * HEADS_DEV * HD * D),
            bytes_accessed=4 << 20,
            transcendentals=HEADS_DEV * TOK * 9 * TOK,
        ),
    )(query_rows, key_rows, value_rows, windows.T, out_weight)


def solution(mesh):
    placed = (P("frame", "head"), P("frame", "head"), P("frame", "head"), P(), P("head", None))
    return jax.shard_map(
        local,
        mesh=mesh,
        in_specs=placed,
        out_specs=P(None, ("frame", "head"), None),
        check_vma=False,
    )
```
